32 devices in a mesh: dp: 4 (over y, core), expert: 2 (over x), tensor: 4 (over z).
Axes of the slice: x: 2, y: 2, z: 4, core: 2. Of those that a mesh axis runs over, the one named last changes fastest.
Arguments:
- tokens: bfloat16 [4096, 1024], P(('dp', 'expert', 'tensor')), may hold values from -6 to 6
- gain_attn: float32 [1024], replicated, may hold values from 0.1 to 1.9
- gain_ffn: float32 [1024], replicated, may hold values from 0.1 to 1.9
- w_query: bfloat16 [1024, 1024], P(None, 'tensor'), may hold values from -0.1875 to 0.1875
- w_key: bfloat16 [1024, 512], P(None, 'tensor'), may hold values from -0.1875 to 0.1875
- w_value: bfloat16 [1024, 512], P(None, 'tensor'), may hold values from -0.1875 to 0.1875
- w_out: bfloat16 [1024, 1024], P('tensor'), may hold values from -1.5 to 1.5
- w_router: bfloat16 [1024, 32], replicated, may hold values from -0.099609375 to 0.099609375
- expert_gate_up: bfloat16 [512, 2, 32, 1024], P(('dp', 'tensor'), None, 'expert'), may hold values from -0.1875 to 0.1875
- expert_down: bfloat16 [512, 32, 1024], P(('dp', 'tensor'), 'expert'), may hold values from -0.75 to 0.75
- segments: int32 [8, 512], P(('dp', 'expert')), may hold values from 0 to 2, as said below
- routes: int32 [4096, 8], P(('dp', 'expert', 'tensor')), may hold values from 0 to 31, all different within a row; in each aligned block of 128 rows (0 to 127, 128 to 255, ...) at most 40 rows name the same one
- cotangent: bfloat16 [4096, 1024], P(('dp', 'expert', 'tensor')), may hold values from -6 to 6
Outputs:
- output: bfloat16 [4096, 1024], P(('dp', 'expert', 'tensor'))
- grad_tokens: float32 [4096, 1024], P(('dp', 'expert', 'tensor'))
- grad_gain_attn: float32 [1024], replicated
- grad_gain_ffn: float32 [1024], replicated
- grad_w_query: float32 [1024, 1024], P(None, 'tensor')
- grad_w_key: float32 [1024, 512], P(None, 'tensor')
- grad_w_value: float32 [1024, 512], P(None, 'tensor')
- grad_w_out: float32 [1024, 1024], P('tensor')
- grad_w_router: float32 [1024, 32], replicated
- grad_gate_up: float32 [512, 2, 32, 1024], P(('dp', 'tensor'), None, 'expert')
- grad_down: float32 [512, 32, 1024], P(('dp', 'tensor'), 'expert')
The draws below stay inside these ranges and needn't reach their ends.
Inputs may be any that keep to these rules, and one draw needn't show every extreme that they name: `routes`: each row names 8 different experts. Among the rows of one device no expert is named by more than 40 rows, a bound that some block reaches. `segments`: segment numbers never fall along a sequence.
All inputs are finite; a program needn't handle non-finite values.
Results may differ from the reference program's by a relative error of at most 0.014.
The reference program's roundings to bfloat16 on the way count: a program that leaves them out, or rounds other values in their place, can miss the bound.
Values may be sent and summed in bfloat16 or wider, within the bound.
No kernel may reach another device: no remote copies, remote signals or barrier semaphores. Data moves between devices by JAX's collectives and lax.ppermute only.
A program may use at most 128 MiB of HBM per device.

```python
import math
import jax
import jax.numpy as jnp
import numpy as np
from jax import lax

D = 1024
HEADS = 16
KV = 8
HD = 64
EXPERTS = 32
TOPK = 8
FF = 512
TOK_DEV = 128
QBLK = 512
LEN = 512
SEQS = 8
TOKENS = 4096
CAPD = 40
N_TENSOR = 4


def draw_segments(key, part):
    key = jax.random.fold_in(key, 11)
    first_key, last_key = jax.random.split(key)
    opening = jax.random.randint(first_key, (SEQS, 1), 0, TOK_DEV)
    closing = jax.random.randint(last_key, (SEQS, 1), LEN - TOK_DEV, LEN)
    places = jnp.arange(LEN, dtype=jnp.int32)[None, :]
    return (places >= opening).astype(jnp.int32) + (places > closing).astype(jnp.int32)


def block_scale(stream_key, shape, cuts, least, top_value):
    loudness, own = 1.0, jax.random.fold_in(stream_key, 6)
    for dim, parts in cuts:
        steps = jnp.exp(jax.random.uniform(jax.random.fold_in(own, dim), (parts,), jnp.float32, least / len(cuts), top_value / len(cuts)))
        loudness = loudness * jnp.repeat(steps, shape[dim] // parts).reshape([-1 if axis == dim else 1 for axis in range(len(shape))])
    return loudness


def routed_block(key, own, number, rows, count, top, limit, slope):
    ranking = jax.random.permutation(key, count)
    heavy_load, common = load_shares(count, rows * top, limit, slope, True), load_shares(count, rows * top, limit, slope, False)
    places = jnp.arange(count)

    def named(tallies, offset_by):
        used = int((tallies > 0).sum())
        fixed = max(1, used // 4)
        moved = fixed + (places - fixed + offset_by * (used - fixed)) % max(1, count - fixed)
        return jnp.zeros((count,), jnp.int32).at[ranking[jnp.where(places < fixed, places, moved)]].set(jnp.asarray(tallies, jnp.int32))

    tallies = jnp.where(number % 4 == 0, named(heavy_load, number // 4), named(common, number - number // 4 - 1))
    mixed = jax.random.permutation(jax.random.fold_in(own, 3), count)
    source_of, receiver = mixed[0:count // 2 * 2:2], mixed[1:count // 2 * 2:2]
    margin = jnp.minimum(tallies[source_of] - 1, limit - tallies[receiver]) // 2
    margin = jnp.where((source_of == ranking[0]) | (receiver == ranking[0]) | (tallies[receiver] == 0), 0, jnp.maximum(margin, 0))
    moved = jax.random.randint(jax.random.fold_in(own, 4), (count // 2,), 0, 1 << 20) % (margin + 1)
    tallies = tallies.at[source_of].add(-moved).at[receiver].add(moved)
    members = jnp.searchsorted(jnp.cumsum(tallies), jnp.arange(rows * top), side="right").astype(jnp.int32)
    grid = members.reshape(top, rows).T
    grid = grid[jax.random.permutation(jax.random.fold_in(own, 1), rows)]
    offset_by = jax.random.randint(jax.random.fold_in(own, 2), (rows, 1), 0, top)
    return jnp.take_along_axis(grid, (jnp.arange(top)[None, :] + offset_by) % top, axis=1)


def load_shares(number_of, total, limit, lean, full):
    portions = [(1 << 20) // math.isqrt(standing ** lean) + 1 for standing in range(1, number_of + 1)]
    largest = limit if full else min(limit, max(-(-total // number_of), total * portions[0] // sum(portions)))
    least = 1 if total - largest >= number_of - 1 else 0
    counts, spare = [largest] + [least] * (number_of - 1), total - largest - least * (number_of - 1)
    while spare > 0:
        candidates = [i for i in range(1, number_of) if counts[i] < largest] or [i for i in range(1, number_of) if counts[i] < limit]
        mass, remaining = sum([portions[i] for i in candidates]), spare
        for i in candidates:
            more = min(limit - counts[i], max(1, remaining * portions[i] // mass), spare)
            counts[i] = counts[i] + more
            spare = spare - more
    return np.array(counts)


def scatter_about(stream_key, dims, scale, most, pieces=(), kind=jnp.bfloat16):
    loudness = block_scale(stream_key, dims, pieces, -0.22, 0.18) if pieces else 1.0
    values = jax.random.normal(stream_key, dims, jnp.float32) * scale * loudness
    return jnp.minimum(jnp.maximum(values, -most), most).astype(kind)


def setup_inputs(seed: int = 0) -> dict:
    key_list = jax.random.split(jax.random.key(seed), 14)
    tokens = scatter_about(key_list[0], (TOKENS, D), 1.0, 6.0, ((0, 32),))
    gain_attn = jnp.clip(1.0 + 0.18 * jax.random.normal(key_list[1], (D,), jnp.float32), 0.1, 1.9)
    gain_ffn = jnp.clip(1.0 + 0.18 * jax.random.normal(key_list[2], (D,), jnp.float32), 0.1, 1.9)
    w_query = scatter_about(key_list[3], (D, HEADS * HD), D ** -0.5, 0.1875, ((1, 4),))
    w_key = scatter_about(key_list[4], (D, KV * HD), D ** -0.5, 0.1875, ((1, 4),))
    w_value = scatter_about(key_list[5], (D, KV * HD), D ** -0.5, 0.1875, ((1, 4),))
    w_out = scatter_about(key_list[6], (HEADS * HD, D), 16 ** -0.5, 1.5, ((0, 4),))
    w_router = scatter_about(key_list[7], (D, EXPERTS), 0.015625, 0.099609375)
    expert_gate_up = scatter_about(key_list[8], (FF, 2, EXPERTS, D), D ** -0.5, 0.1875, ((0, 16), (2, 2)))
    expert_down = scatter_about(key_list[9], (FF, EXPERTS, D), 64 ** -0.5, 0.75, ((0, 16), (1, 2)))
    segments = draw_segments(jax.random.fold_in(key_list[13], 71), 0)
    routes_keys = jax.random.split(jax.random.fold_in(key_list[11], 1), TOKENS // TOK_DEV)
    routes_turns = jax.random.permutation(jax.random.fold_in(key_list[11], 3), TOKENS // TOK_DEV)
    routes = jax.vmap(lambda own, number: routed_block(jax.random.fold_in(key_list[11], 2), own, number, TOK_DEV, EXPERTS, TOPK, CAPD, 1))(routes_keys, routes_turns).reshape((TOKENS, TOPK))
    cotangent = scatter_about(key_list[12], (TOKENS, D), 1.0, 6.0, ((0, 32),))
    return dict(tokens=tokens, gain_attn=gain_attn, gain_ffn=gain_ffn, w_query=w_query, w_key=w_key, w_value=w_value, w_out=w_out, w_router=w_router, expert_gate_up=expert_gate_up, expert_down=expert_down, segments=segments, routes=routes, cotangent=cotangent)


@jax.custom_vjp
def low(v):
    return lax.optimization_barrier(v.astype(jnp.bfloat16)).astype(jnp.float32)

@jax.custom_vjp
def low_back(v):
    return v

def low_keep(v):
    return (low(v), None)

def low_pass(kept, grad):
    return (grad,)

def back_keep(v):
    return (v, None)

def back_low(kept, grad):
    return (low(grad),)
low.defvjp(low_keep, low_pass)
low_back.defvjp(back_keep, back_low)
epsilon = 1e-06

def matmul(left, right):
    return jnp.dot(left, right, precision=lax.Precision.HIGHEST, preferred_element_type=jnp.float32)

def contract(formula, left, right):
    return jnp.einsum(formula, left, right, precision=lax.Precision.HIGHEST, preferred_element_type=jnp.float32)

def rms_scale(values):
    return lax.rsqrt(lax.optimization_barrier(jnp.mean(values * values, axis=-1, keepdims=True)) + epsilon)

def positions_of(segment_row):
    places = jnp.arange(segment_row.shape[0], dtype=jnp.int32)
    boundary = jnp.concatenate([jnp.ones((1,), dtype=jnp.bool_), segment_row[1:] != segment_row[:-1]])
    opening = lax.cummax(jnp.where(boundary, places, 0), axis=0)
    return (places - opening).astype(jnp.float32)

def rotary_tables(positions, head_size):
    half_size = head_size // 2
    frequency = jnp.power(10000.0, -2.0 * jnp.arange(half_size, dtype=jnp.float32) / head_size)
    angles = positions[:, None] * frequency[None, :]
    return (jnp.cos(angles)[:, None, :], jnp.sin(angles)[:, None, :])

def rotate(values, cosine, sine):
    half_size = values.shape[-1] // 2
    former = values[..., :half_size]
    latter = values[..., half_size:]
    return jnp.concatenate([former * cosine - latter * sine, latter * cosine + former * sine], axis=-1)

def attention_sequence(normed, segment_row, w_query, w_key, w_value, w_out):
    length = normed.shape[0]
    group_size = HEADS // KV
    scale = HD ** (-0.5)
    cosine, sine = rotary_tables(positions_of(segment_row), HD)
    query_lin = low_back(matmul(normed, w_query)).reshape(length, HEADS, HD)
    key_lin = low_back(matmul(normed, w_key)).reshape(length, KV, HD)
    values = low(low_back(matmul(normed, w_value))).reshape(length, KV, HD)
    queries = low(rotate(query_lin, cosine, sine)).reshape(length, KV, group_size, HD)
    keys = low(rotate(key_lin, cosine, sine))
    places = jnp.arange(length, dtype=jnp.int32)

    def one_block(block_index):
        offset = block_index * QBLK
        block_rows = lax.dynamic_slice_in_dim(queries, offset, QBLK, 0)
        row_places = offset + jnp.arange(QBLK, dtype=jnp.int32)
        row_segments = lax.dynamic_slice_in_dim(segment_row, offset, QBLK, 0)
        allowed = (row_segments[:, None] == segment_row[None, :]) & (places[None, :] <= row_places[:, None])
        scores = low_back(contract('qkgd,skd->kgqs', block_rows, keys) * scale)
        masked = jnp.where(allowed, scores, -1e+30)
        shifted = jnp.exp(masked - lax.optimization_barrier(jnp.max(masked, axis=-1, keepdims=True)))
        weights = low(shifted / lax.optimization_barrier(jnp.sum(shifted, axis=-1, keepdims=True)))
        return contract('kgqs,skd->qkgd', weights, values)
    block_out = lax.map(jax.checkpoint(one_block), jnp.arange(length // QBLK, dtype=jnp.int32))
    mixed = low(low_back(block_out.reshape(length, HEADS * HD)))
    return low_back(matmul(mixed, w_out))

def experts_sequence(normed, routes, w_router, gate_up, down):
    length, width = normed.shape
    logits = matmul(normed, w_router)
    chosen = jnp.take_along_axis(logits, routes, axis=1)
    gates = jax.nn.softmax(chosen, axis=-1)
    capacity = CAPD * N_TENSOR
    places = jnp.arange(length, dtype=jnp.int32)
    padded = jnp.concatenate([normed, jnp.zeros((1, width), jnp.float32)], axis=0)
    padded_gates = jnp.zeros((1,), jnp.float32)

    def one_expert(summed, expert):
        matches = routes == expert
        present = jnp.any(matches, axis=1)
        gate_value = lax.optimization_barrier(jnp.sum(jnp.where(matches, gates, 0.0), axis=1))
        rank_value = jnp.cumsum(present.astype(jnp.int32), dtype=jnp.int32) - 1
        slot_table = jnp.full((capacity,), length, jnp.int32).at[jnp.where(present, rank_value, capacity)].set(places, mode='drop')
        slot_rows = low_back(padded[slot_table])
        weights_in = lax.dynamic_index_in_dim(gate_up, expert, 2, keepdims=False)
        weights_out = lax.dynamic_index_in_dim(down, expert, 1, keepdims=False)
        gate_part = low_back(contract('rd,fd->rf', slot_rows, weights_in[:, 0]))
        up_part = low_back(contract('rd,fd->rf', slot_rows, weights_in[:, 1]))
        active = low(jax.nn.silu(gate_part) * up_part)
        expert_rows = low(low_back(matmul(active, weights_out)))
        slot_gates = jnp.concatenate([gate_value, padded_gates])[slot_table]
        return (summed.at[slot_table].add(slot_gates[:, None] * expert_rows), None)
    summed, unused = lax.scan(jax.checkpoint(one_expert), jnp.zeros((length + 1, width), jnp.float32), jnp.arange(EXPERTS, dtype=jnp.int32))
    return summed[:length]

def layer_sequence(source, params, segment_row, route_rows):
    gain_attn, gain_ffn, w_query, w_key, w_value, w_out, w_router, gate_up, down = params
    normed = low(source * rms_scale(source) * gain_attn)
    hidden = source + attention_sequence(normed, segment_row, w_query, w_key, w_value, w_out)
    normed_ffn = low(hidden * rms_scale(hidden) * gain_ffn)
    return hidden + experts_sequence(normed_ffn, route_rows, w_router, gate_up, down)

def reference(tokens, gain_attn, gain_ffn, w_query, w_key, w_value, w_out, w_router, expert_gate_up, expert_down, segments, routes, cotangent):
    weights = tuple((array.astype(jnp.float32) for array in (gain_attn, gain_ffn, w_query, w_key, w_value, w_out, w_router, expert_gate_up, expert_down)))
    token_seqs = tokens.reshape(SEQS, LEN, D)
    cot_seqs = cotangent.reshape(SEQS, LEN, D)
    route_seqs = routes.reshape(SEQS, LEN, TOPK)

    def one_sequence(totals, scanned):
        token_seq, cot_seq, segment_seq, route_seq = scanned

        def forward(source, *params):
            return layer_sequence(source, params, segment_seq, route_seq)
        result, pullback = jax.vjp(forward, token_seq.astype(jnp.float32), *weights)
        gradients = pullback(cot_seq.astype(jnp.float32))
        totals = tuple((running + added for running, added in zip(totals, gradients[1:])))
        return (totals, (result.astype(jnp.bfloat16), gradients[0]))
    initial = tuple((jnp.zeros_like(array) for array in weights))
    totals, (outputs, token_grads) = lax.scan(one_sequence, initial, (token_seqs, cot_seqs, segments, route_seqs))
    return (outputs.reshape(TOKENS, D), token_grads.reshape(TOKENS, D), totals[0], totals[1], totals[2], totals[3], totals[4], totals[5], totals[6], totals[7], totals[8])
```

```python
import functools

import jax
import jax.numpy as jnp
from jax import lax
from jax.experimental import pallas as pl
from jax.experimental.pallas import tpu as pltpu
from jax.sharding import PartitionSpec as P

HD = 64
QBLK = 512
LANES = 128


epsilon = 1e-06


def rms_scale(values):
    return lax.rsqrt(jnp.mean(values * values, axis=-1, keepdims=True) + epsilon)


def positions_of(segment_row):
    places = jnp.arange(segment_row.shape[0], dtype=jnp.int32)
    boundary = jnp.concatenate(
        [jnp.ones((1,), dtype=jnp.bool_), segment_row[1:] != segment_row[:-1]]
    )
    opening = lax.cummax(jnp.where(boundary, places, 0), axis=0)
    return (places - opening).astype(jnp.float32)


def rotary_tables(positions, head_size):
    half_size = head_size // 2
    frequency = jnp.power(10000.0, -2.0 * jnp.arange(half_size, dtype=jnp.float32) / head_size)
    angles = positions[:, None] * frequency[None, :]
    return (jnp.cos(angles)[:, None, :], jnp.sin(angles)[:, None, :])


def rotate(values, cosine, sine):
    half_size = values.shape[-1] // 2
    former = values[..., :half_size]
    latter = values[..., half_size:]
    return jnp.concatenate(
        [former * cosine - latter * sine, latter * cosine + former * sine], axis=-1
    )


def rotate_back(gradient, cosine, sine):
    half_size = gradient.shape[-1] // 2
    former = gradient[..., :half_size]
    latter = gradient[..., half_size:]
    return jnp.concatenate(
        [former * cosine + latter * sine, latter * cosine - former * sine], axis=-1
    )


def norm_back(values, scale, gain, grad_normed):
    weighted = grad_normed * gain
    inner = jnp.sum(weighted * values, axis=-1, keepdims=True)
    grad_values = scale * weighted - values * (scale * scale * scale) * inner / values.shape[-1]
    grad_gain = jnp.sum(grad_normed * values * scale, axis=0)
    return (grad_values, grad_gain)


def swap(values, axis, mask):
    size = lax.axis_size(axis)
    return lax.ppermute(values, axis, [(place, place ^ mask) for place in range(size)])


def together(arrays):
    return list(lax.optimization_barrier(tuple(arrays)))


def axis_steps():
    tensor_step = ("tensor", tuple(range(1, lax.axis_size("tensor"))))
    expert_step = ("expert", tuple(range(1, lax.axis_size("expert"))))
    near = ("dp", (1,))
    far = ("dp", tuple(range(2, lax.axis_size("dp"), 2)))
    return tensor_step, expert_step, far, near


def held_by(order):
    index = 0
    for axis, masks in reversed(order):
        index = index * (len(masks) + 1) + (lax.axis_index(axis) // masks[0]) % (len(masks) + 1)
    return index


def in_held_order(values, order, rows):
    own = held_by(order)
    return jnp.concatenate(
        [
            lax.dynamic_slice_in_dim(values, (own ^ place) * rows, rows, 0)
            for place in range(values.shape[0] // rows)
        ],
        axis=0,
    )


def gather_parts(parts, orders):
    parts = list(parts)
    for step in range(len(orders[0])):
        arrived = []
        for part, order in zip(parts, orders):
            axis, masks = order[step]
            arrived.append([swap(part, axis, mask) for mask in masks])
        flat = together([piece for pieces in arrived for piece in pieces])
        joined, at = [], 0
        for part, pieces in zip(parts, arrived):
            joined.append(jnp.concatenate([part] + flat[at : at + len(pieces)], axis=0))
            at += len(pieces)
        parts = together(joined)
    return parts


def scatter_parts(parts, orders):
    parts = list(parts)
    steps = len(orders[0])
    for step in reversed(range(steps)):
        kept, arrived = [], []
        for part, order in zip(parts, orders):
            axis, masks = order[step]
            rows = part.shape[0] // (len(masks) + 1)
            sent = part.astype(jnp.bfloat16)
            kept.append(part[:rows])
            arrived.append(
                [
                    swap(sent[(place + 1) * rows : (place + 2) * rows], axis, mask)
                    for place, mask in enumerate(masks)
                ]
            )
        flat = together([piece for pieces in arrived for piece in pieces])
        summed, at = [], 0
        for part, pieces in zip(kept, arrived):
            total = part.astype(jnp.float32)
            for piece in flat[at : at + len(pieces)]:
                total = total + piece.astype(jnp.float32)
            at += len(pieces)
            summed.append(total if step == 0 else total.astype(jnp.bfloat16))
        parts = together(summed)
    return parts


def sum_everywhere(values):
    for axis in ("dp", "expert", "tensor"):
        mask = 1
        while mask < lax.axis_size(axis):
            values = values + swap(values, axis, mask)
            mask *= 2
    return values


def dot_rows(left, right):
    return lax.dot_general(
        left, right, (((1,), (1,)), ((), ())), preferred_element_type=jnp.float32
    )


def dot_tokens(left, right):
    return lax.dot_general(
        left, right, (((0,), (0,)), ((), ())), preferred_element_type=jnp.float32
    )


def moe_kernel(
    local_experts,
    first_ref,
    rows_ref,
    cot_ref,
    router_ref,
    left_ref,
    right_ref,
    mixture_ref,
    grad_rows_ref,
    grad_left_ref,
    grad_right_ref,
    grad_router_ref,
    gates_ref,
    gate_grads_ref,
    mixture_sum_ref,
    grad_rows_sum_ref,
):
    block = pl.program_id(0)
    width = rows_ref.shape[1]
    units = left_ref.shape[2]

    @pl.when(block == 0)
    def begin():
        picked = cot_ref[:, width:].astype(jnp.float32)
        logits = jnp.dot(rows_ref[...], router_ref[...], preferred_element_type=jnp.float32)
        masked = jnp.where(picked > 0.0, logits, -1e30)
        powers = jnp.exp(masked - jnp.max(masked, axis=1, keepdims=True)) * picked
        gates_ref[...] = powers / jnp.sum(powers, axis=1, keepdims=True)
        gate_grads_ref[...] = jnp.zeros_like(gate_grads_ref)
        mixture_sum_ref[...] = jnp.zeros_like(mixture_sum_ref)
        grad_rows_sum_ref[...] = jnp.zeros_like(grad_rows_sum_ref)

    first = first_ref[block]
    lane = lax.broadcasted_iota(jnp.int32, gates_ref.shape, 1)
    here = (lane >= first) & (lane < first + local_experts)

    def fold(values):
        shift = local_experts
        while shift < LANES:
            values = values + pltpu.roll(values, shift, 1)
            shift *= 2
        return values

    unit_gates = jnp.concatenate(
        [fold(jnp.where(here, gates_ref[...], 0.0))] * (units // LANES), axis=1
    )
    rows = rows_ref[...]
    cot = cot_ref[:, :width]
    for part_ref, grad_ref in ((left_ref, grad_left_ref), (right_ref, grad_right_ref)):
        gate_part = dot_rows(rows, part_ref[0, 0])
        up_part = dot_rows(rows, part_ref[0, 1])
        cot_active = dot_rows(cot, part_ref[0, 2])
        sigma = jax.nn.sigmoid(gate_part)
        silu = gate_part * sigma
        active = silu * up_part
        gated = (active * unit_gates).astype(jnp.bfloat16)
        products = active * cot_active
        summed = products[:, :LANES]
        for place in range(1, units // LANES):
            summed = summed + products[:, place * LANES : (place + 1) * LANES]
        gate_grads_ref[...] += jnp.where(here, fold(summed), 0.0)
        grad_active = cot_active * unit_gates
        grad_up = (grad_active * silu).astype(jnp.bfloat16)
        grad_gate = (grad_active * up_part * sigma * (1.0 + gate_part * (1.0 - sigma))).astype(
            jnp.bfloat16
        )
        mixture_sum_ref[...] += jnp.dot(
            gated, part_ref[0, 2], preferred_element_type=jnp.float32
        )
        grad_rows_sum_ref[...] += jnp.dot(
            grad_gate, part_ref[0, 0], preferred_element_type=jnp.float32
        ) + jnp.dot(grad_up, part_ref[0, 1], preferred_element_type=jnp.float32)
        grad_ref[0, 0] = dot_tokens(grad_gate, rows).astype(jnp.bfloat16)
        grad_ref[0, 1] = dot_tokens(grad_up, rows).astype(jnp.bfloat16)
        grad_ref[0, 2] = dot_tokens(gated, cot).astype(jnp.bfloat16)

    @pl.when(block == pl.num_programs(0) - 1)
    def finish():
        gates = gates_ref[...]
        gate_grads = gate_grads_ref[...]
        mean_grad = jnp.sum(gates * gate_grads, axis=1, keepdims=True)
        logit_grads = gates * (gate_grads - mean_grad)
        coarse = logit_grads.astype(jnp.bfloat16).astype(jnp.float32)
        logit_pair = (coarse + pltpu.roll(logit_grads - coarse, LANES // 2, 1)).astype(
            jnp.bfloat16
        )
        mixture_ref[...] = mixture_sum_ref[...].astype(jnp.bfloat16)
        grad_rows_ref[...] = (
            grad_rows_sum_ref[...] + dot_rows(logit_pair, router_ref[...])
        ).astype(jnp.bfloat16)
        grad_router_ref[...] = dot_tokens(logit_pair, rows)


def experts_of_rows(rows, cot, router, left, right, firsts, local_experts, turned):
    count, width = rows.shape
    blocks, kinds, units, unused = left.shape
    fixed = lambda block, first_ref: (0, 0)
    mine = lambda block, first_ref: (block, 0, 0, 0)
    crossed = lambda block, first_ref: (turned(block), 0, 0, 0)
    once = pl.Buffered(1)
    return pl.pallas_call(
        functools.partial(moe_kernel, local_experts),
        grid_spec=pltpu.PrefetchScalarGridSpec(
            num_scalar_prefetch=1,
            grid=(blocks,),
            in_specs=[
                pl.BlockSpec((count, width), fixed, pipeline_mode=once),
                pl.BlockSpec((count, width + LANES), fixed, pipeline_mode=once),
                pl.BlockSpec((width, LANES), fixed, pipeline_mode=once),
                pl.BlockSpec((1, kinds, units, width), mine),
                pl.BlockSpec((1, kinds, units, width), crossed),
            ],
            out_specs=[
                pl.BlockSpec((count, width), fixed, pipeline_mode=once),
                pl.BlockSpec((count, width), fixed, pipeline_mode=once),
                pl.BlockSpec((1, kinds, units, width), mine),
                pl.BlockSpec((1, kinds, units, width), crossed),
                pl.BlockSpec((LANES, width), fixed, pipeline_mode=once),
            ],
            scratch_shapes=[
                pltpu.VMEM((count, LANES), jnp.float32),
                pltpu.VMEM((count, LANES), jnp.float32),
                pltpu.VMEM((count, width), jnp.float32),
                pltpu.VMEM((count, width), jnp.float32),
            ],
        ),
        out_shape=[
            jax.ShapeDtypeStruct((count, width), jnp.bfloat16),
            jax.ShapeDtypeStruct((count, width), jnp.bfloat16),
            jax.ShapeDtypeStruct(left.shape, jnp.bfloat16),
            jax.ShapeDtypeStruct(right.shape, jnp.bfloat16),
            jax.ShapeDtypeStruct((LANES, width), jnp.float32),
        ],
        compiler_params=pltpu.CompilerParams(
            dimension_semantics=("arbitrary",), vmem_limit_bytes=60 * 2**20
        ),
        cost_estimate=pl.CostEstimate(
            flops=36 * count * blocks * units * width,
            bytes_accessed=blocks * units * width * 24 + count * width * 8,
            transcendentals=2 * count * blocks * units,
        ),
    )(firsts, rows, cot, router, left, right)

def on_device(
    tokens,
    gain_attn,
    gain_ffn,
    w_query,
    w_key,
    w_value,
    w_out,
    w_router,
    expert_gate_up,
    expert_down,
    segments,
    routes,
    cotangent,
):
    row_count, model_width = tokens.shape
    top_count = routes.shape[1]
    expert_count = w_router.shape[1]
    query_heads = w_query.shape[1] // HD
    kv_heads = w_key.shape[1] // HD
    group_size = query_heads // kv_heads
    scale = HD ** (-0.5)
    highest = lax.Precision.HIGHEST
    source = tokens.astype(jnp.float32)
    scale_attn = rms_scale(source)
    normed = (source * scale_attn * gain_attn).astype(jnp.bfloat16)
    tensor_step, expert_step, far, near = axis_steps()
    tensor_order = [tensor_step]
    token_order = [tensor_step, near]
    weight_orders = [[expert_step, far], [far, expert_step]]

    expert_ids = jnp.arange(expert_count, dtype=jnp.int32)
    picks = jnp.sum(
        (routes[:, :, None] == expert_ids[None, None, :]).astype(jnp.bfloat16), axis=1
    )
    cot_picks = jnp.concatenate(
        [cotangent, picks, jnp.zeros((row_count, LANES - expert_count), jnp.bfloat16)], axis=1
    )
    unit_rows, local_experts = expert_down.shape[:2]
    half = unit_rows // 2
    units = half * local_experts
    expert_parts = []
    for low in (0, half):
        taken = expert_gate_up[low : low + half]
        expert_parts.append(
            jnp.stack(
                [taken[:, 0], taken[:, 1], expert_down[low : low + half]], axis=0
            ).reshape(1, 3, units, model_width)
        )
    left, right = gather_parts(expert_parts, weight_orders)
    spare_units = -units % LANES
    if spare_units:
        left, right = (
            jnp.pad(part, ((0, 0), (0, 0), (0, spare_units), (0, 0))) for part in (left, right)
        )
    expert_size, far_size = len(expert_step[1]) + 1, len(far[1]) + 1
    first_experts = jnp.stack(
        [
            (lax.axis_index("expert") ^ (block % expert_size)) * local_experts
            for block in range(expert_size * far_size)
        ]
    ).astype(jnp.int32)
    unused = jnp.zeros((model_width, LANES // 2 - expert_count), jnp.bfloat16)
    router_pair = jnp.concatenate([w_router, unused, w_router, unused], axis=1)

    def sum_over_sequences(values, orders):
        parts = jnp.split(values, len(orders), axis=0)
        count = lax.axis_size("dp") * lax.axis_size("expert")
        rows = parts[0].shape[0] // count
        parts = [in_held_order(part, order, rows) for part, order in zip(parts, orders)]
        shares = [share.astype(jnp.bfloat16) for share in scatter_parts(parts, orders)]
        parts = gather_parts(shares, orders)
        parts = [in_held_order(part, order, rows) for part, order in zip(parts, orders)]
        return jnp.concatenate(parts, axis=0).astype(jnp.float32)

    (sequence,) = gather_parts([normed], [tensor_order])
    sequence, cot_picks = lax.optimization_barrier((sequence, cot_picks))
    (cot_rows,) = gather_parts([cot_picks], [token_order])
    length = sequence.shape[0]
    positions = positions_of(segments[0])
    segment_row = in_held_order(segments[0], tensor_order, row_count)
    cosine, sine = rotary_tables(in_held_order(positions, tensor_order, row_count), HD)
    query_lin = jnp.dot(sequence, w_query, preferred_element_type=jnp.float32).reshape(
        length, query_heads, HD
    )
    key_lin = jnp.dot(sequence, w_key, preferred_element_type=jnp.float32).reshape(
        length, kv_heads, HD
    )
    values = (
        jnp.dot(sequence, w_value, preferred_element_type=jnp.float32)
        .astype(jnp.bfloat16)
        .reshape(length, kv_heads, HD)
    )
    queries = (
        rotate(query_lin, cosine, sine)
        .astype(jnp.bfloat16)
        .reshape(length, kv_heads, group_size, HD)
    )
    keys = rotate(key_lin, cosine, sine).astype(jnp.bfloat16)
    places = in_held_order(
        jnp.arange(length, dtype=jnp.int32), tensor_order, row_count
    )

    def block_scores(offset):
        block_rows = lax.dynamic_slice_in_dim(queries, offset, QBLK, 0)
        row_places = lax.dynamic_slice_in_dim(places, offset, QBLK, 0)
        row_segments = lax.dynamic_slice_in_dim(segment_row, offset, QBLK, 0)
        allowed = (row_segments[:, None] == segment_row[None, :]) & (
            places[None, :] <= row_places[:, None]
        )
        scores = (
            jnp.einsum("qkgd,skd->kgqs", block_rows, keys, preferred_element_type=jnp.float32)
            * scale
        )
        return (block_rows, jnp.where(allowed, scores, -1e30))

    def forward_block(block_index):
        block_rows, masked = block_scores(block_index * QBLK)
        peak = jnp.max(masked, axis=-1, keepdims=True)
        shifted = jnp.exp(masked - peak)
        summed = jnp.sum(shifted, axis=-1, keepdims=True)
        weights = (shifted / summed).astype(jnp.bfloat16)
        mixed_block = jnp.einsum(
            "kgqs,skd->qkgd", weights, values, preferred_element_type=jnp.float32
        )
        return (mixed_block.astype(jnp.bfloat16), (peak + jnp.log(summed))[..., 0])

    block_ids = jnp.arange(length // QBLK, dtype=jnp.int32)
    mixed_blocks, log_totals = lax.map(forward_block, block_ids)
    mixed = mixed_blocks.reshape(length, query_heads * HD)
    (attended,) = scatter_parts(
        [jnp.dot(mixed, w_out, preferred_element_type=jnp.float32)], [tensor_order]
    )
    hidden = source + attended
    scale_ffn = rms_scale(hidden)
    normed_ffn = (hidden * scale_ffn * gain_ffn).astype(jnp.bfloat16)
    (rows,) = gather_parts([normed_ffn], [token_order])
    mixture_part, grad_rows_part, grad_left, grad_right, grad_router_rows = experts_of_rows(
        rows,
        cot_rows,
        router_pair,
        left,
        right,
        first_experts,
        local_experts,
        lambda block: (block % expert_size) * far_size + block // expert_size,
    )
    (grad_normed_ffn,) = scatter_parts([grad_rows_part], [token_order])
    grad_parts = scatter_parts([grad_left[:, :, :units], grad_right[:, :, :units]], weight_orders)
    grad_left, grad_right = (
        part.reshape(3, half, local_experts, model_width) for part in grad_parts
    )
    grad_gate_up = jnp.concatenate(
        [jnp.stack([part[0], part[1]], axis=1) for part in (grad_left, grad_right)], axis=0
    )
    grad_down = jnp.concatenate([grad_left[2], grad_right[2]], axis=0)
    grad_output = cotangent.astype(jnp.float32)
    grad_hidden_norm, grad_gain_ffn = norm_back(hidden, scale_ffn, gain_ffn, grad_normed_ffn)
    grad_hidden = grad_output + grad_hidden_norm
    (attn_grad,) = gather_parts([grad_hidden.astype(jnp.bfloat16)], [tensor_order])
    attn_grad, mixture_part = lax.optimization_barrier((attn_grad, mixture_part))
    (mixture,) = scatter_parts([mixture_part], [token_order])
    output = (hidden + mixture).astype(jnp.bfloat16)
    grad_router = sum_everywhere(
        grad_router_rows[:expert_count]
        + grad_router_rows[LANES // 2 : LANES // 2 + expert_count]
    ).T
    grad_w_out = jnp.einsum("lh,ld->hd", mixed, attn_grad, preferred_element_type=jnp.float32)
    grad_w_out = sum_over_sequences(grad_w_out, [[expert_step, far, near]])
    grad_mixed = (
        jnp.einsum("ld,hd->lh", attn_grad, w_out, preferred_element_type=jnp.float32)
        .astype(jnp.bfloat16)
        .reshape(length, kv_heads, group_size, HD)
    )

    def backward_block(carried, scanned):
        key_sum, value_sum = carried
        block_index, log_block = scanned
        offset = block_index * QBLK
        block_rows, masked = block_scores(offset)
        probs = jnp.exp(masked - log_block[..., None])
        weights = probs.astype(jnp.bfloat16)
        grad_block = lax.dynamic_slice_in_dim(grad_mixed, offset, QBLK, 0)
        grad_probs = jnp.einsum(
            "qkgd,skd->kgqs", grad_block, values, preferred_element_type=jnp.float32
        )
        inner = jnp.sum(probs * grad_probs, axis=-1, keepdims=True)
        grad_scores = (probs * (grad_probs - inner)).astype(jnp.bfloat16)
        grad_query = (
            jnp.einsum("kgqs,skd->qkgd", grad_scores, keys, preferred_element_type=jnp.float32)
            * scale
        )
        key_sum = (
            key_sum
            + jnp.einsum(
                "kgqs,qkgd->skd", grad_scores, block_rows, preferred_element_type=jnp.float32
            )
            * scale
        )
        value_sum = value_sum + jnp.einsum(
            "kgqs,qkgd->skd", weights, grad_block, preferred_element_type=jnp.float32
        )
        return ((key_sum, value_sum), grad_query)

    zero_keys = jnp.zeros((length, kv_heads, HD), jnp.float32)
    (key_grads, value_grads), query_grads = lax.scan(
        backward_block, (zero_keys, zero_keys), (block_ids, log_totals)
    )
    grad_query_lin = (
        rotate_back(query_grads.reshape(length, query_heads, HD), cosine, sine)
        .astype(jnp.bfloat16)
        .reshape(length, query_heads * HD)
    )
    grad_key_lin = (
        rotate_back(key_grads, cosine, sine).astype(jnp.bfloat16).reshape(length, kv_heads * HD)
    )
    grad_value_lin = value_grads.astype(jnp.bfloat16).reshape(length, kv_heads * HD)
    grad_w_query = jnp.einsum(
        "ld,lh->dh", sequence, grad_query_lin, preferred_element_type=jnp.float32
    )
    grad_w_key = jnp.einsum("ld,lh->dh", sequence, grad_key_lin, preferred_element_type=jnp.float32)
    grad_w_value = jnp.einsum(
        "ld,lh->dh", sequence, grad_value_lin, preferred_element_type=jnp.float32
    )
    grad_sequence = (
        jnp.einsum("lh,dh->ld", grad_query_lin, w_query, preferred_element_type=jnp.float32)
        + jnp.einsum("lh,dh->ld", grad_key_lin, w_key, preferred_element_type=jnp.float32)
        + jnp.einsum("lh,dh->ld", grad_value_lin, w_value, preferred_element_type=jnp.float32)
    )
    (grad_normed,) = scatter_parts([grad_sequence], [tensor_order])
    grad_source_norm, grad_gain_attn = norm_back(source, scale_attn, gain_attn, grad_normed)
    grad_tokens = grad_hidden + grad_source_norm
    grad_w_query, grad_w_key, grad_w_value = jnp.split(
        sum_over_sequences(
            jnp.concatenate([grad_w_query, grad_w_key, grad_w_value], axis=1),
            [[expert_step, far, near], [far, expert_step, near]],
        ),
        (w_query.shape[1], w_query.shape[1] + w_key.shape[1]),
        axis=1,
    )
    grad_gains = sum_everywhere(jnp.stack([grad_gain_attn, grad_gain_ffn]))
    grad_gain_attn, grad_gain_ffn = grad_gains[0], grad_gains[1]
    return (
        output,
        grad_tokens,
        grad_gain_attn,
        grad_gain_ffn,
        grad_w_query,
        grad_w_key,
        grad_w_value,
        grad_w_out,
        grad_router,
        grad_gate_up,
        grad_down,
    )


def solution(mesh):
    placed = (
        P(("dp", "expert", "tensor"), None),
        P(),
        P(),
        P(None, "tensor"),
        P(None, "tensor"),
        P(None, "tensor"),
        P("tensor", None),
        P(),
        P(("dp", "tensor"), None, "expert", None),
        P(("dp", "tensor"), "expert", None),
        P(("dp", "expert"), None),
        P(("dp", "expert", "tensor"), None),
        P(("dp", "expert", "tensor"), None),
    )
    return jax.shard_map(
        on_device,
        mesh=mesh,
        in_specs=placed,
        out_specs=(
            P(("dp", "expert", "tensor"), None),
            P(("dp", "expert", "tensor"), None),
            P(),
            P(),
            P(None, "tensor"),
            P(None, "tensor"),
            P(None, "tensor"),
            P("tensor", None),
            P(),
            P(("dp", "tensor"), None, "expert", None),
            P(("dp", "tensor"), "expert", None),
        ),
        check_vma=False,
    )
```

```python
import functools

import jax
import jax.numpy as jnp
from jax import lax
from jax.experimental import pallas as pl
from jax.experimental.pallas import tpu as pltpu
from jax.sharding import PartitionSpec as P

HD = 64
QBLK = 512
LANES = 128
TOKEN_ROWS = 512


epsilon = 1e-06


def rms_scale(values):
    return lax.rsqrt(jnp.mean(values * values, axis=-1, keepdims=True) + epsilon)


def positions_of(segment_row):
    places = jnp.arange(segment_row.shape[0], dtype=jnp.int32)
    boundary = jnp.concatenate(
        [jnp.ones((1,), dtype=jnp.bool_), segment_row[1:] != segment_row[:-1]]
    )
    opening = lax.cummax(jnp.where(boundary, places, 0), axis=0)
    return (places - opening).astype(jnp.float32)


def rotary_tables(positions, head_size):
    half_size = head_size // 2
    frequency = jnp.power(10000.0, -2.0 * jnp.arange(half_size, dtype=jnp.float32) / head_size)
    angles = positions[:, None] * frequency[None, :]
    return (jnp.cos(angles)[:, None, :], jnp.sin(angles)[:, None, :])


def rotate(values, cosine, sine):
    half_size = values.shape[-1] // 2
    former = values[..., :half_size]
    latter = values[..., half_size:]
    return jnp.concatenate(
        [former * cosine - latter * sine, latter * cosine + former * sine], axis=-1
    )


def rotate_back(gradient, cosine, sine):
    half_size = gradient.shape[-1] // 2
    former = gradient[..., :half_size]
    latter = gradient[..., half_size:]
    return jnp.concatenate(
        [former * cosine + latter * sine, latter * cosine - former * sine], axis=-1
    )


def norm_back(values, scale, gain, grad_normed):
    weighted = grad_normed * gain
    inner = jnp.sum(weighted * values, axis=-1, keepdims=True)
    grad_values = scale * weighted - values * (scale * scale * scale) * inner / values.shape[-1]
    grad_gain = jnp.sum(grad_normed * values * scale, axis=0)
    return (grad_values, grad_gain)


def swap(values, axis, mask):
    size = lax.axis_size(axis)
    return lax.ppermute(values, axis, [(place, place ^ mask) for place in range(size)])


def together(arrays):
    return list(lax.optimization_barrier(tuple(arrays)))


def tie(*trees):
    return lax.optimization_barrier(trees)


def axis_steps():
    tensor_step = ("tensor", tuple(range(1, lax.axis_size("tensor"))))
    expert_step = ("expert", tuple(range(1, lax.axis_size("expert"))))
    near = ("dp", (1,))
    far = ("dp", tuple(range(2, lax.axis_size("dp"), 2)))
    return tensor_step, expert_step, far, near


def held_by(order):
    index = 0
    for axis, masks in reversed(order):
        index = index * (len(masks) + 1) + (lax.axis_index(axis) // masks[0]) % (len(masks) + 1)
    return index


def in_held_order(values, order, rows):
    own = held_by(order)
    return jnp.concatenate(
        [
            lax.dynamic_slice_in_dim(values, (own ^ place) * rows, rows, 0)
            for place in range(values.shape[0] // rows)
        ],
        axis=0,
    )


def gather_parts(parts, orders):
    parts = list(parts)
    for step in range(len(orders[0])):
        arrived = []
        for part, order in zip(parts, orders):
            axis, masks = order[step]
            arrived.append([swap(part, axis, mask) for mask in masks])
        flat = together([piece for pieces in arrived for piece in pieces])
        joined, at = [], 0
        for part, pieces in zip(parts, arrived):
            joined.append(jnp.concatenate([part] + flat[at : at + len(pieces)], axis=0))
            at += len(pieces)
        parts = together(joined)
    return parts


def send_sums(parts, orders, step):
    kept, arrived = [], []
    for part, order in zip(parts, orders):
        axis, masks = order[step]
        rows = part.shape[0] // (len(masks) + 1)
        sent = part.astype(jnp.bfloat16)
        kept.append(part[:rows])
        arrived.append(
            [
                swap(sent[(place + 1) * rows : (place + 2) * rows], axis, mask)
                for place, mask in enumerate(masks)
            ]
        )
    return kept, arrived


def added(parts):
    return sum(part.astype(jnp.float32) for part in parts)


def take_sums(kept, arrived):
    return [
        added([part] + pieces).astype(jnp.bfloat16) for part, pieces in zip(kept, arrived)
    ]


def send_parts(parts, orders, step):
    return [
        [swap(part, order[step][0], mask) for mask in order[step][1]]
        for part, order in zip(parts, orders)
    ]


def take_parts(parts, arrived):
    return [
        jnp.concatenate([part] + pieces, axis=0) for part, pieces in zip(parts, arrived)
    ]


def scatter_parts(parts, orders):
    for step in reversed(range(len(orders[0]))):
        kept, arrived = send_sums(parts, orders, step)
        (arrived,) = tie(arrived)
        parts = take_sums(kept, arrived) if step else [
            added([part] + pieces) for part, pieces in zip(kept, arrived)
        ]
    return parts


def axis_masks(axis):
    return [1 << bit for bit in range((lax.axis_size(axis) - 1).bit_length())]


def sum_over(values, axis, masks):
    for mask in masks:
        values = values + swap(values, axis, mask)
    return values


def dot_rows(left, right):
    return lax.dot_general(
        left, right, (((1,), (1,)), ((), ())), preferred_element_type=jnp.float32
    )


def dot_tokens(left, right):
    return lax.dot_general(
        left, right, (((0,), (0,)), ((), ())), preferred_element_type=jnp.float32
    )


def expert_kernel(local_experts, size, where, array_count, token_places, refs):
    first_ref, owner_ref, router_ref, refs = refs[0], refs[1], refs[2], refs[3:]
    token_pieces, refs = refs[: len(token_places)], refs[len(token_places) :]
    arrays, refs = refs[:array_count], refs[array_count:]
    pieces = [arrays[place].at[index] for place, index in where]
    step_count = len(pieces) // 2
    outs, refs = refs[:6], refs[6:]
    grads_ref = outs[5]
    (
        gates_ref,
        gate_grads_ref,
        mixture_sum_ref,
        grad_sum_ref,
        weights_ref,
        lin_grads_ref,
        made_ref,
        tokens_ref,
        copy_sems,
        out_sems,
        token_sems,
    ) = refs
    sum_refs = (mixture_sum_ref, grad_sum_ref, gate_grads_ref)
    step = pl.program_id(0)
    slot = lax.rem(step, 2)
    count = tokens_ref.shape[0]
    block = count // 2
    width = router_ref.shape[0]
    units = weights_ref.shape[3]
    pair = 2 * units
    sub = min(block, TOKEN_ROWS)
    spans = [
        (part, low, part * block + low) for part in range(2) for low in range(0, block, sub)
    ]
    token_copies = [
        pltpu.make_async_copy(
            piece,
            tokens_ref.at[
                pl.ds(row, piece.shape[0]), pl.ds(column * width, piece.shape[1])
            ],
            token_sems.at[place],
        )
        for place, (piece, (row, column)) in enumerate(zip(token_pieces, token_places))
    ]

    def copy_in(piece, member, to_slot):
        return pltpu.make_async_copy(
            pieces[piece],
            weights_ref.at[to_slot, :, member, pl.ds(0, size), :],
            copy_sems.at[to_slot, member],
        )

    def copy_out(from_slot, member, owner):
        return pltpu.make_async_copy(
            made_ref.at[from_slot, member, :, pl.ds(0, size), :],
            grads_ref.at[owner],
            out_sems.at[from_slot, member],
        )

    @pl.when(step == 0)
    def begin():
        if size < units:
            weights_ref[...] = jnp.zeros_like(weights_ref)
        copy_in(0, 0, 0).start()
        copy_in(1, 1, 0).start()
        for token_copy in token_copies:
            token_copy.start()
        for sum_ref in sum_refs:
            sum_ref[...] = jnp.zeros_like(sum_ref)
        for token_copy in token_copies:
            token_copy.wait()
        for part, low, base in spans:
            picked = tokens_ref[pl.ds(base, sub), 2 * width :].astype(jnp.float32)
            logits = jnp.dot(
                tokens_ref[pl.ds(base, sub), :width],
                router_ref[...],
                preferred_element_type=jnp.float32,
            )
            masked = jnp.where(picked > 0.0, logits, -1e30)
            powers = jnp.exp(masked - jnp.max(masked, axis=1, keepdims=True)) * picked
            gates_ref[pl.ds(base, sub), :] = powers / jnp.sum(powers, axis=1, keepdims=True)

    for later in range(1, step_count):

        @pl.when(step == later - 1)
        def fetch(later=later):
            copy_in(2 * later, 0, later % 2).start()
            copy_in(2 * later + 1, 1, later % 2).start()

    for member in range(2):
        copy_in(0, member, slot).wait()

    firsts = [first_ref[2 * step + member] for member in range(2)]
    lane = lax.broadcasted_iota(jnp.int32, (sub, LANES), 1)
    heres = [(lane >= first) & (lane < first + local_experts) for first in firsts]

    def fold(values):
        shift = local_experts
        while shift < LANES:
            values = values + pltpu.roll(values, shift, 1)
            shift *= 2
        return values

    gate_up = weights_ref[slot, pl.ds(0, 2)].reshape(2 * pair, width)
    down = weights_ref[slot, 2].reshape(pair, width)
    for part, low, base in spans:
        span = pl.ds(base, sub)
        rows = tokens_ref[span, :width]
        cot = tokens_ref[span, width : 2 * width]
        gates = gates_ref[span, :]
        unit_gates = jnp.concatenate(
            [
                part_gates
                for here in heres
                for part_gates in [fold(jnp.where(here, gates, 0.0))] * (units // LANES)
            ],
            axis=1,
        )
        lin = dot_rows(rows, gate_up)
        gate_part, up_part = lin[:, :pair], lin[:, pair:]
        cot_active = dot_rows(cot, down)
        sigma = jax.nn.sigmoid(gate_part)
        silu = gate_part * sigma
        active = silu * up_part
        gated = (active * unit_gates).astype(jnp.bfloat16)
        products = active * cot_active
        for member, here in enumerate(heres):
            summed = 0.0
            for place in range(member * units, (member + 1) * units, LANES):
                summed = summed + products[:, place : place + LANES]
            gate_grads_ref[span, :] += jnp.where(here, fold(summed), 0.0)
        grad_active = cot_active * unit_gates
        grad_up = (grad_active * silu).astype(jnp.bfloat16)
        grad_gate = (grad_active * up_part * (sigma + silu * (1.0 - sigma))).astype(
            jnp.bfloat16
        )
        grad_lin = jnp.concatenate([grad_gate, grad_up], axis=1)
        lin_grads_ref[span, pl.ds(0, 2 * pair)] = grad_lin
        lin_grads_ref[span, pl.ds(2 * pair, pair)] = gated
        mixture_sum_ref[span, :] += jnp.dot(gated, down, preferred_element_type=jnp.float32)
        grad_sum_ref[span, :] += jnp.dot(
            grad_lin, gate_up, preferred_element_type=jnp.float32
        )

    @pl.when(step >= 2)
    def reuse():
        for member in range(2):
            copy_out(slot, member, 0).wait()

    def weight_grad(column, columns, side):
        return dot_tokens(
            lin_grads_ref[:, pl.ds(column, columns)],
            tokens_ref[:, side * width : (side + 1) * width],
        ).astype(jnp.bfloat16)

    for kind in range(3):
        made = weight_grad(kind * pair, pair, int(kind == 2))
        for member in range(2):
            made_ref[slot, member, kind] = made[member * units : (member + 1) * units]
    for member in range(2):
        copy_out(slot, member, owner_ref[2 * step + member]).start()

    @pl.when(step == step_count - 1)
    def finish():
        mixture_refs, grad_rows_refs, grad_router_ref = outs[:2], outs[2:4], outs[4]
        total = jnp.zeros(grad_router_ref.shape, jnp.float32)
        for part, low, base in spans:
            span = pl.ds(base, sub)
            gates = gates_ref[span, :]
            gate_grads = gate_grads_ref[span, :]
            mean_grad = jnp.sum(gates * gate_grads, axis=1, keepdims=True)
            logit_grads = gates * (gate_grads - mean_grad)
            coarse = logit_grads.astype(jnp.bfloat16).astype(jnp.float32)
            logit_pair = (coarse + pltpu.roll(logit_grads - coarse, LANES // 2, 1)).astype(
                jnp.bfloat16
            )
            mixture_refs[part][pl.ds(low, sub), :] = mixture_sum_ref[span, :].astype(jnp.bfloat16)
            grad_rows_refs[part][pl.ds(low, sub), :] = (
                grad_sum_ref[span, :] + dot_rows(logit_pair, router_ref[...])
            ).astype(jnp.bfloat16)
            total = total + dot_tokens(logit_pair, tokens_ref[span, :width])
        grad_router_ref[...] = total
        for member in range(2):
            copy_out(slot, member, 0).wait()
        if step_count > 1:
            for member in range(2):
                copy_out(1 - slot, member, 0).wait()


def experts_of_rows(token_pieces, token_places, count, router, arrays, where, firsts, owners, local_experts):
    block = count // 2
    width = router.shape[0]
    piece_count = len(where)
    size = arrays[0].shape[2]
    units = -(-size // LANES) * LANES
    anywhere = pl.BlockSpec(memory_space=pl.ANY)
    whole = lambda shape: pl.BlockSpec(
        shape, lambda *indices: (0,) * len(shape), pipeline_mode=pl.Buffered(1)
    )
    return pl.pallas_call(
        lambda *refs: expert_kernel(
            local_experts, size, where, len(arrays), token_places, refs
        ),
        grid_spec=pltpu.PrefetchScalarGridSpec(
            num_scalar_prefetch=2,
            grid=(piece_count // 2,),
            in_specs=[
                whole((width, LANES)),
            ]
            + [anywhere] * (len(token_pieces) + len(arrays)),
            out_specs=[whole((block, width))] * 4 + [whole((LANES, width)), anywhere],
            scratch_shapes=[
                pltpu.VMEM((count, LANES), jnp.float32),
                pltpu.VMEM((count, LANES), jnp.float32),
                pltpu.VMEM((count, width), jnp.float32),
                pltpu.VMEM((count, width), jnp.float32),
                pltpu.VMEM((2, 3, 2, units, width), jnp.bfloat16),
                pltpu.VMEM((count, 6 * units), jnp.bfloat16),
                pltpu.VMEM((2, 2, 3, units, width), jnp.bfloat16),
                pltpu.VMEM((count, 2 * width + LANES), jnp.bfloat16),
                pltpu.SemaphoreType.DMA((2, 2)),
                pltpu.SemaphoreType.DMA((2, 2)),
                pltpu.SemaphoreType.DMA((len(token_pieces),)),
            ],
        ),
        out_shape=[
            *[jax.ShapeDtypeStruct((block, width), jnp.bfloat16)] * 4,
            jax.ShapeDtypeStruct((LANES, width), jnp.float32),
            jax.ShapeDtypeStruct((piece_count, 3, size, width), jnp.bfloat16),
        ],
        compiler_params=pltpu.CompilerParams(
            dimension_semantics=("arbitrary",), vmem_limit_bytes=60 * 2**20
        ),
        cost_estimate=pl.CostEstimate(
            flops=18 * count * piece_count * units * width,
            bytes_accessed=piece_count * units * width * 12 + count * width * 16,
            transcendentals=count * piece_count * units,
        ),
    )(firsts, owners, router, *token_pieces, *arrays)


def spread_sums(parts, places, piece_count, shapes):
    held_rows, columns = parts[0][0].shape
    part_rows = held_rows * len(parts[0])
    rows = part_rows // piece_count
    upper = shapes[0][0] // 2
    lower = shapes[3][0]
    per_part = (part_rows - upper) // lower

    def kernel(places_ref, *refs):
        inputs, outputs, held_ref = refs[:-5], refs[-5:-1], refs[-1]
        for part in range(2):
            for place in range(len(parts[0])):
                held_ref[pl.ds(place * held_rows, held_rows), :] = inputs[
                    part * len(parts[0]) + place
                ][...].astype(jnp.float32)
            own = places_ref[part]

            def taken(low, high):
                pieces = []
                for piece in range(low // rows, -(-high // rows)):
                    start = pl.multiple_of((own ^ piece) * rows, 8)
                    whole_piece = held_ref[pl.ds(start, rows), :]
                    pieces.append(
                        whole_piece[
                            max(low - piece * rows, 0) : min(high - piece * rows, rows)
                        ]
                    )
                return jnp.concatenate(pieces, axis=0)

            top = taken(0, upper)
            at = 0
            for output in outputs[:3]:
                wide = output.shape[1]
                output[pl.ds(part * upper, upper), :] = top[:, at : at + wide]
                at += wide
            for place in range(per_part):
                start = upper + place * lower
                column = (part * per_part + place) * columns
                outputs[3][:, pl.ds(column, columns)] = taken(start, start + lower)

    inputs = [piece for part in parts for piece in part]
    whole = pl.BlockSpec(memory_space=pltpu.VMEM)
    return pl.pallas_call(
        kernel,
        in_specs=[pl.BlockSpec(memory_space=pltpu.SMEM)] + [whole] * len(inputs),
        out_specs=[whole] * 4,
        out_shape=[jax.ShapeDtypeStruct(shape, jnp.float32) for shape in shapes],
        scratch_shapes=[pltpu.VMEM((part_rows, columns), jnp.float32)],
        compiler_params=pltpu.CompilerParams(vmem_limit_bytes=32 * 2**20),
        cost_estimate=pl.CostEstimate(
            flops=0, bytes_accessed=12 * part_rows * columns, transcendentals=0
        ),
    )(places, *inputs)


def spread_units(sums, gate_up_shape, down_shape):
    unit_rows, local_experts, width = down_shape
    if local_experts % 8:
        sums = sums.reshape(2, 3, unit_rows // 2, local_experts, width).astype(jnp.float32)
        grad_gate_up = jnp.moveaxis(sums[:, :2], 1, 2).reshape(gate_up_shape)
        return grad_gate_up, sums[:, 2].reshape(down_shape)
    split = 4
    block = unit_rows // 2 // split

    def kernel(sums_ref, gate_up_ref, down_ref):
        shape = (block, local_experts, width)
        for kind in range(2):
            gate_up_ref[:, kind] = sums_ref[0, kind].astype(jnp.float32).reshape(shape)
        down_ref[...] = sums_ref[0, 2].astype(jnp.float32).reshape(shape)

    return pl.pallas_call(
        kernel,
        grid=(2 * split,),
        in_specs=[
            pl.BlockSpec(
                (1, 3, block * local_experts, width),
                lambda step: (step // split, 0, step % split, 0),
            )
        ],
        out_specs=[
            pl.BlockSpec((block, 2, local_experts, width), lambda step: (step, 0, 0, 0)),
            pl.BlockSpec((block, local_experts, width), lambda step: (step, 0, 0)),
        ],
        out_shape=[
            jax.ShapeDtypeStruct(gate_up_shape, jnp.float32),
            jax.ShapeDtypeStruct(down_shape, jnp.float32),
        ],
        compiler_params=pltpu.CompilerParams(
            dimension_semantics=("arbitrary",), vmem_limit_bytes=32 * 2**20
        ),
        cost_estimate=pl.CostEstimate(
            flops=0, bytes_accessed=18 * unit_rows * local_experts * width, transcendentals=0
        ),
    )(sums)


def on_device(
    tokens,
    gain_attn,
    gain_ffn,
    w_query,
    w_key,
    w_value,
    w_out,
    w_router,
    expert_gate_up,
    expert_down,
    segments,
    routes,
    cotangent,
):
    row_count, model_width = tokens.shape
    top_count = routes.shape[1]
    expert_count = w_router.shape[1]
    query_heads = w_query.shape[1] // HD
    kv_heads = w_key.shape[1] // HD
    group_size = query_heads // kv_heads
    scale = HD ** (-0.5)
    highest = lax.Precision.HIGHEST
    source = tokens.astype(jnp.float32)
    scale_attn = rms_scale(source)
    normed = (source * scale_attn * gain_attn).astype(jnp.bfloat16)
    tensor_step, expert_step, far, near = axis_steps()
    tensor_order = [tensor_step]
    token_order = [tensor_step, near]
    expert_masks, far_masks = (0,) + expert_step[1], (0,) + far[1]
    partners = [(mask, other) for other in far_masks for mask in expert_masks]

    expert_ids = jnp.arange(expert_count, dtype=jnp.int32)
    picks = jnp.sum(
        (routes[:, :, None] == expert_ids[None, None, :]).astype(jnp.bfloat16), axis=1
    )
    cot_picks = jnp.concatenate(
        [cotangent, picks, jnp.zeros((row_count, LANES - expert_count), jnp.bfloat16)], axis=1
    )
    unit_rows, local_experts = expert_down.shape[:2]
    half = unit_rows // 2
    units = half * local_experts
    expert_parts = []
    for low in (0, half):
        taken = expert_gate_up[low : low + half]
        expert_parts.append(
            jnp.stack(
                [taken[:, 0], taken[:, 1], expert_down[low : low + half]], axis=0
            ).reshape(1, 3, units, model_width)
        )
    first_parts = [
        [part] + [swap(part, axis, mask) for mask in masks[1:]]
        for part, axis, masks in zip(
            expert_parts, ("expert", "dp"), (expert_masks, far_masks)
        )
    ]
    dp_size, expert_size = lax.axis_size("dp"), lax.axis_size("expert")
    unused = jnp.zeros((model_width, LANES // 2 - expert_count), jnp.bfloat16)
    router_pair = jnp.concatenate([w_router, unused, w_router, unused], axis=1)

    (sequence,) = gather_parts([normed], [tensor_order])
    sequence, cot_picks, router_pair = lax.optimization_barrier(
        (sequence, cot_picks, router_pair)
    )
    first_mask, later_masks = tensor_step[1][0], tensor_step[1][1:]
    cot_first = swap(cot_picks, "tensor", first_mask)
    length = sequence.shape[0]
    positions = positions_of(segments[0])
    segment_row = in_held_order(segments[0], tensor_order, row_count)
    cosine, sine = rotary_tables(in_held_order(positions, tensor_order, row_count), HD)
    query_lin = jnp.dot(sequence, w_query, preferred_element_type=jnp.float32).reshape(
        length, query_heads, HD
    )
    key_lin = jnp.dot(sequence, w_key, preferred_element_type=jnp.float32).reshape(
        length, kv_heads, HD
    )
    values = (
        jnp.dot(sequence, w_value, preferred_element_type=jnp.float32)
        .astype(jnp.bfloat16)
        .reshape(length, kv_heads, HD)
    )
    queries = (
        rotate(query_lin, cosine, sine)
        .astype(jnp.bfloat16)
        .reshape(length, kv_heads, group_size, HD)
    )
    keys = rotate(key_lin, cosine, sine).astype(jnp.bfloat16)
    places = in_held_order(
        jnp.arange(length, dtype=jnp.int32), tensor_order, row_count
    )

    def block_scores(offset):
        block_rows = lax.dynamic_slice_in_dim(queries, offset, QBLK, 0)
        row_places = lax.dynamic_slice_in_dim(places, offset, QBLK, 0)
        row_segments = lax.dynamic_slice_in_dim(segment_row, offset, QBLK, 0)
        allowed = (row_segments[:, None] == segment_row[None, :]) & (
            places[None, :] <= row_places[:, None]
        )
        scores = (
            jnp.einsum("qkgd,skd->kgqs", block_rows, keys, preferred_element_type=jnp.float32)
            * scale
        )
        return (block_rows, jnp.where(allowed, scores, -1e30))

    def forward_block(block_index):
        block_rows, masked = block_scores(block_index * QBLK)
        peak = jnp.max(masked, axis=-1, keepdims=True)
        shifted = jnp.exp(masked - peak)
        summed = jnp.sum(shifted, axis=-1, keepdims=True)
        weights = (shifted / summed).astype(jnp.bfloat16)
        mixed_block = jnp.einsum(
            "kgqs,skd->qkgd", weights, values, preferred_element_type=jnp.float32
        )
        return (mixed_block.astype(jnp.bfloat16), (peak + jnp.log(summed))[..., 0])

    block_ids = jnp.arange(length // QBLK, dtype=jnp.int32)
    mixed_blocks, log_totals = lax.map(forward_block, block_ids)
    mixed, cot_first = tie(mixed_blocks.reshape(length, query_heads * HD), cot_first)
    attended_parts = jnp.dot(mixed, w_out, preferred_element_type=jnp.float32)
    kept, arrived = send_sums([attended_parts], [tensor_order], 0)
    arrived = arrived[0]
    arrived[0], first_parts = tie(arrived[0], first_parts)
    joined_parts = [jnp.concatenate(parts, axis=0) for parts in first_parts]
    arrived[1:], joined_parts = tie(arrived[1:], joined_parts)
    attended = added([kept[0]] + arrived)
    weight_arrays, where = [], [{}, {}]
    for side, (masks, next_axis, next_masks) in enumerate(
        ((expert_masks, "dp", far_masks), (far_masks, "expert", expert_masks))
    ):
        name = lambda mask, other: (mask, other) if side == 0 else (other, mask)
        for mask, part in zip(masks, first_parts[side]):
            where[side][name(mask, 0)] = (len(weight_arrays), 0)
            weight_arrays.append(part)
        joined = joined_parts[side]
        for other in next_masks[1:]:
            for index, mask in enumerate(masks):
                where[side][name(mask, other)] = (len(weight_arrays), index)
            weight_arrays.append(swap(joined, next_axis, other))
    hidden = source + attended
    scale_ffn = rms_scale(hidden)
    normed_ffn = (hidden * scale_ffn * gain_ffn).astype(jnp.bfloat16)
    own_tokens = jnp.concatenate([normed_ffn, cot_picks], axis=1)
    arrived = [swap(normed_ffn, "tensor", first_mask)] + [
        swap(own_tokens, "tensor", mask) for mask in later_masks
    ]
    (arrived,) = tie(arrived)
    near_pieces = [normed_ffn, cot_picks, arrived[0], cot_first] + arrived[1:]
    near_places = [(0, 0), (0, 1), (row_count, 0), (row_count, 1)] + [
        (place * row_count, 0) for place in range(2, len(tensor_step[1]) + 1)
    ]
    pair_rows = (len(tensor_step[1]) + 1) * row_count
    token_pieces = near_pieces + [swap(piece, "dp", 1) for piece in near_pieces]
    token_places = near_places + [(row + pair_rows, column) for row, column in near_places]
    held, firsts, owners = [], [], []
    for mask, other in partners:
        owner_expert = lax.axis_index("expert") ^ mask
        owner_place = (lax.axis_index("dp") ^ other) // 2
        for side in range(2):
            held.append(where[side][mask, other])
            firsts.append(owner_expert * local_experts)
            owners.append((owner_place * expert_size + owner_expert) * 2 + side)
    *mixture_part, grad_near, grad_far, grad_router_rows, grad_pieces = experts_of_rows(
        token_pieces,
        token_places,
        2 * pair_rows,
        router_pair,
        weight_arrays,
        held,
        jnp.stack(firsts).astype(jnp.int32),
        jnp.stack(owners).astype(jnp.int32),
        local_experts,
    )
    groups = [
        [
            place * expert_size + other
            for place in range(start, dp_size, 2)
            for other in range(expert_size)
        ]
        for start in range(2)
    ]
    grad_units = lax.psum_scatter(
        grad_pieces,
        ("dp", "expert"),
        scatter_dimension=0,
        tiled=True,
        axis_index_groups=groups,
    )
    near_rows = added([grad_near, swap(grad_far, "dp", 1)]).astype(jnp.bfloat16)
    grad_router = (
        grad_router_rows[:expert_count]
        + grad_router_rows[LANES // 2 : LANES // 2 + expert_count]
    )
    kept, arrived = send_sums([near_rows], [tensor_order], 0)
    (arrived,) = tie(arrived)
    grad_normed_ffn = added([kept[0]] + arrived[0])
    grad_output = cotangent.astype(jnp.float32)
    grad_hidden_norm, grad_gain_ffn = norm_back(hidden, scale_ffn, gain_ffn, grad_normed_ffn)
    grad_hidden = grad_output + grad_hidden_norm
    attn_rows = grad_hidden.astype(jnp.bfloat16)
    arrived = send_parts([attn_rows], [tensor_order], 0)
    (arrived,) = tie(arrived)
    (attn_grad,) = take_parts([attn_rows], arrived)
    mixture_part, attn_grad = tie(mixture_part, attn_grad)
    mixture_rows = added([mixture_part[0], swap(mixture_part[1], "dp", 1)]).astype(
        jnp.bfloat16
    )
    tensor_masks = axis_masks("tensor")
    grad_router = sum_over(grad_router, "tensor", tensor_masks)
    grad_w_out = jnp.einsum("lh,ld->hd", mixed, attn_grad, preferred_element_type=jnp.float32)
    grad_mixed = (
        jnp.einsum("ld,hd->lh", attn_grad, w_out, preferred_element_type=jnp.float32)
        .astype(jnp.bfloat16)
        .reshape(length, kv_heads, group_size, HD)
    )

    def backward_block(carried, scanned):
        key_sum, value_sum = carried
        block_index, log_block = scanned
        offset = block_index * QBLK
        block_rows, masked = block_scores(offset)
        probs = jnp.exp(masked - log_block[..., None])
        weights = probs.astype(jnp.bfloat16)
        grad_block = lax.dynamic_slice_in_dim(grad_mixed, offset, QBLK, 0)
        grad_probs = jnp.einsum(
            "qkgd,skd->kgqs", grad_block, values, preferred_element_type=jnp.float32
        )
        inner = jnp.sum(probs * grad_probs, axis=-1, keepdims=True)
        grad_scores = (probs * (grad_probs - inner)).astype(jnp.bfloat16)
        grad_query = (
            jnp.einsum("kgqs,skd->qkgd", grad_scores, keys, preferred_element_type=jnp.float32)
            * scale
        )
        key_sum = (
            key_sum
            + jnp.einsum(
                "kgqs,qkgd->skd", grad_scores, block_rows, preferred_element_type=jnp.float32
            )
            * scale
        )
        value_sum = value_sum + jnp.einsum(
            "kgqs,qkgd->skd", weights, grad_block, preferred_element_type=jnp.float32
        )
        return ((key_sum, value_sum), grad_query)

    zero_keys = jnp.zeros((length, kv_heads, HD), jnp.float32)
    (key_grads, value_grads), query_grads = lax.scan(
        backward_block, (zero_keys, zero_keys), (block_ids, log_totals)
    )
    grad_query_lin = (
        rotate_back(query_grads.reshape(length, query_heads, HD), cosine, sine)
        .astype(jnp.bfloat16)
        .reshape(length, query_heads * HD)
    )
    grad_key_lin = (
        rotate_back(key_grads, cosine, sine).astype(jnp.bfloat16).reshape(length, kv_heads * HD)
    )
    grad_value_lin = value_grads.astype(jnp.bfloat16).reshape(length, kv_heads * HD)
    grad_w_query = jnp.einsum(
        "ld,lh->dh", sequence, grad_query_lin, preferred_element_type=jnp.float32
    )
    grad_w_key = jnp.einsum("ld,lh->dh", sequence, grad_key_lin, preferred_element_type=jnp.float32)
    grad_w_value = jnp.einsum(
        "ld,lh->dh", sequence, grad_value_lin, preferred_element_type=jnp.float32
    )
    grad_sequence = (
        jnp.einsum("lh,dh->ld", grad_query_lin, w_query, preferred_element_type=jnp.float32)
        + jnp.einsum("lh,dh->ld", grad_key_lin, w_key, preferred_element_type=jnp.float32)
        + jnp.einsum("lh,dh->ld", grad_value_lin, w_value, preferred_element_type=jnp.float32)
    )
    sequence_rows = grad_sequence.astype(jnp.bfloat16)
    gain_sums = jnp.stack(
        [
            jnp.sum(grad_sequence * sequence.astype(jnp.float32), axis=0) / gain_attn,
            grad_gain_ffn,
        ]
    )
    columns = jnp.concatenate([grad_w_query, grad_w_key, grad_w_value], axis=1)
    sum_orders = [[expert_step, far, near], [far, expert_step, near]]
    sequence_count = lax.axis_size("dp") * lax.axis_size("expert")

    def reorder(parts):
        return [
            in_held_order(part, order, part.shape[0] // sequence_count)
            for part, order in zip(parts, sum_orders)
        ]

    sequence_rows, mixture_rows, columns, grad_w_out, gain_sums, grad_router = tie(
        sequence_rows, mixture_rows, columns, grad_w_out, gain_sums, grad_router
    )
    kept, arrived = send_sums([sequence_rows], [tensor_order], 0)
    arrived = arrived[0]
    mixture_kept, mixture_arrived = send_sums([mixture_rows], [tensor_order], 0)
    mixture_arrived = mixture_arrived[0]
    blocks_out = jnp.split(grad_w_out, model_width // columns.shape[1], axis=1)
    block_rows, per_part = blocks_out[0].shape[0], len(blocks_out) // 2
    sums = reorder(
        [
            jnp.concatenate([upper] + lower, axis=0)
            for upper, lower in zip(
                jnp.split(columns, 2, axis=0), (blocks_out[:per_part], blocks_out[per_part:])
            )
        ]
    )
    loose = jnp.concatenate([grad_router, gain_sums], axis=0)
    for step in reversed(range(3)):
        sums_kept, sums_arrived = send_sums(sums, sum_orders, step)
        loose = sum_over(
            loose,
            ("expert", "dp", "dp")[step],
            (axis_masks("expert"), axis_masks("dp")[1:], axis_masks("dp")[:1])[step],
        )
        if step == 2:
            sums_arrived, loose = tie(sums_arrived, loose)
        elif step == 1:
            sums_arrived, loose, arrived[0] = tie(sums_arrived, loose, arrived[0])
        else:
            sums_arrived, loose, arrived = tie(sums_arrived, loose, arrived)
        sums = take_sums(sums_kept, sums_arrived)
    grad_router, gain_sums = loose[:expert_count].T, loose[expert_count:]
    for step in range(3):
        sums_arrived = send_parts(sums, sum_orders, step)
        if step == 0:
            gain_sums = sum_over(gain_sums, "tensor", tensor_masks)
            sums_arrived, gain_sums, mixture_arrived[0] = tie(
                sums_arrived, gain_sums, mixture_arrived[0]
            )
        elif step == 1:
            sums_arrived, mixture_arrived, grad_units = tie(
                sums_arrived, mixture_arrived, grad_units
            )
        if step < 2:
            sums = take_parts(sums, sums_arrived)
    grad_gain_attn, grad_gain_ffn = gain_sums[0], gain_sums[1]
    grad_w_query, grad_w_key, grad_w_value, grad_w_out = spread_sums(
        [[part] + pieces for part, pieces in zip(sums, sums_arrived)],
        jnp.stack([held_by(order) for order in sum_orders]).astype(jnp.int32),
        sequence_count,
        [w_query.shape, w_key.shape, w_value.shape, w_out.shape],
    )
    grad_normed = added([grad_sequence[:row_count]] + arrived)
    output = (hidden + added(mixture_kept + mixture_arrived)).astype(jnp.bfloat16)
    grad_source_norm, unused_gain = norm_back(source, scale_attn, gain_attn, grad_normed)
    grad_tokens = grad_hidden + grad_source_norm
    grad_gate_up, grad_down = spread_units(
        grad_units, expert_gate_up.shape, expert_down.shape
    )
    return (
        output,
        grad_tokens,
        grad_gain_attn,
        grad_gain_ffn,
        grad_w_query,
        grad_w_key,
        grad_w_value,
        grad_w_out,
        grad_router,
        grad_gate_up,
        grad_down,
    )


def solution(mesh):
    placed = (
        P(("dp", "expert", "tensor"), None),
        P(),
        P(),
        P(None, "tensor"),
        P(None, "tensor"),
        P(None, "tensor"),
        P("tensor", None),
        P(),
        P(("dp", "tensor"), None, "expert", None),
        P(("dp", "tensor"), "expert", None),
        P(("dp", "expert"), None),
        P(("dp", "expert", "tensor"), None),
        P(("dp", "expert", "tensor"), None),
    )
    return jax.shard_map(
        on_device,
        mesh=mesh,
        in_specs=placed,
        out_specs=(
            P(("dp", "expert", "tensor"), None),
            P(("dp", "expert", "tensor"), None),
            P(),
            P(),
            P(None, "tensor"),
            P(None, "tensor"),
            P(None, "tensor"),
            P("tensor", None),
            P(),
            P(("dp", "tensor"), None, "expert", None),
            P(("dp", "tensor"), "expert", None),
        ),
        check_vma=False,
    )
```

```python
import functools

import jax
import jax.numpy as jnp
from jax import lax
from jax.experimental import pallas as pl
from jax.experimental.pallas import tpu as pltpu
from jax.sharding import PartitionSpec as P

HD = 64
QBLK = 512
LANES = 128
TOKEN_ROWS = 256


epsilon = 1e-06


def rms_scale(values):
    return lax.rsqrt(jnp.mean(values * values, axis=-1, keepdims=True) + epsilon)


def positions_of(segment_row):
    places = jnp.arange(segment_row.shape[0], dtype=jnp.int32)
    boundary = jnp.concatenate(
        [jnp.ones((1,), dtype=jnp.bool_), segment_row[1:] != segment_row[:-1]]
    )
    opening = lax.cummax(jnp.where(boundary, places, 0), axis=0)
    return (places - opening).astype(jnp.float32)


def rotary_tables(positions, head_size):
    half_size = head_size // 2
    frequency = jnp.power(10000.0, -2.0 * jnp.arange(half_size, dtype=jnp.float32) / head_size)
    angles = positions[:, None] * frequency[None, :]
    return (jnp.cos(angles)[:, None, :], jnp.sin(angles)[:, None, :])


def rotate(values, cosine, sine):
    half_size = values.shape[-1] // 2
    former = values[..., :half_size]
    latter = values[..., half_size:]
    return jnp.concatenate(
        [former * cosine - latter * sine, latter * cosine + former * sine], axis=-1
    )


def rotate_back(gradient, cosine, sine):
    half_size = gradient.shape[-1] // 2
    former = gradient[..., :half_size]
    latter = gradient[..., half_size:]
    return jnp.concatenate(
        [former * cosine + latter * sine, latter * cosine - former * sine], axis=-1
    )


def norm_back(values, scale, gain, grad_normed):
    weighted = grad_normed * gain
    inner = jnp.sum(weighted * values, axis=-1, keepdims=True)
    grad_values = scale * weighted - values * (scale * scale * scale) * inner / values.shape[-1]
    grad_gain = jnp.sum(grad_normed * values * scale, axis=0)
    return (grad_values, grad_gain)


def swap(values, axis, mask):
    size = lax.axis_size(axis)
    return lax.ppermute(values, axis, [(place, place ^ mask) for place in range(size)])


def together(arrays):
    return list(lax.optimization_barrier(tuple(arrays)))


def tie(*trees):
    return lax.optimization_barrier(trees)


def axis_steps():
    tensor_step = ("tensor", tuple(range(1, lax.axis_size("tensor"))))
    expert_step = ("expert", tuple(range(1, lax.axis_size("expert"))))
    near = ("dp", (1,))
    far = ("dp", tuple(range(2, lax.axis_size("dp"), 2)))
    return tensor_step, expert_step, far, near


def held_by(order):
    index = 0
    for axis, masks in reversed(order):
        index = index * (len(masks) + 1) + (lax.axis_index(axis) // masks[0]) % (len(masks) + 1)
    return index


def in_held_order(values, order, rows):
    own = held_by(order)
    return jnp.concatenate(
        [
            lax.dynamic_slice_in_dim(values, (own ^ place) * rows, rows, 0)
            for place in range(values.shape[0] // rows)
        ],
        axis=0,
    )


def gather_parts(parts, orders):
    parts = list(parts)
    for step in range(len(orders[0])):
        arrived = []
        for part, order in zip(parts, orders):
            axis, masks = order[step]
            arrived.append([swap(part, axis, mask) for mask in masks])
        flat = together([piece for pieces in arrived for piece in pieces])
        joined, at = [], 0
        for part, pieces in zip(parts, arrived):
            joined.append(jnp.concatenate([part] + flat[at : at + len(pieces)], axis=0))
            at += len(pieces)
        parts = together(joined)
    return parts


def send_sums(parts, orders, step):
    kept, arrived = [], []
    for part, order in zip(parts, orders):
        axis, masks = order[step]
        rows = part.shape[0] // (len(masks) + 1)
        sent = part.astype(jnp.bfloat16)
        kept.append(part[:rows])
        arrived.append(
            [
                swap(sent[(place + 1) * rows : (place + 2) * rows], axis, mask)
                for place, mask in enumerate(masks)
            ]
        )
    return kept, arrived


def added(parts):
    return sum(part.astype(jnp.float32) for part in parts)


def take_sums(kept, arrived):
    return [
        added([part] + pieces).astype(jnp.bfloat16) for part, pieces in zip(kept, arrived)
    ]


def send_parts(parts, orders, step):
    return [
        [swap(part, order[step][0], mask) for mask in order[step][1]]
        for part, order in zip(parts, orders)
    ]


def take_parts(parts, arrived):
    return [
        jnp.concatenate([part] + pieces, axis=0) for part, pieces in zip(parts, arrived)
    ]


def scatter_parts(parts, orders):
    for step in reversed(range(len(orders[0]))):
        kept, arrived = send_sums(parts, orders, step)
        (arrived,) = tie(arrived)
        parts = take_sums(kept, arrived) if step else [
            added([part] + pieces) for part, pieces in zip(kept, arrived)
        ]
    return parts


def axis_masks(axis):
    return [1 << bit for bit in range((lax.axis_size(axis) - 1).bit_length())]


def sum_over(values, axis, masks):
    for mask in masks:
        values = values + swap(values, axis, mask)
    return values


def dot_rows(left, right):
    return lax.dot_general(
        left, right, (((1,), (1,)), ((), ())), preferred_element_type=jnp.float32
    )


def dot_tokens(left, right):
    return lax.dot_general(
        left, right, (((0,), (0,)), ((), ())), preferred_element_type=jnp.float32
    )


def expert_kernel(local_experts, size, where, array_count, token_places, refs):
    first_ref, owner_ref, router_ref, refs = refs[0], refs[1], refs[2], refs[3:]
    token_pieces, refs = refs[: len(token_places)], refs[len(token_places) :]
    arrays, refs = refs[:array_count], refs[array_count:]
    pieces = [arrays[place].at[index] for place, index in where]
    step_count = len(pieces) // 2
    outs, refs = refs[:6], refs[6:]
    grads_ref = outs[5]
    (
        gates_ref,
        gate_grads_ref,
        mixture_sum_ref,
        grad_sum_ref,
        weights_ref,
        lin_grads_ref,
        made_ref,
        tokens_ref,
        copy_sems,
        out_sems,
        token_sems,
    ) = refs
    sum_refs = (mixture_sum_ref, grad_sum_ref, gate_grads_ref)
    step = pl.program_id(0)
    slot = lax.rem(step, 2)
    count = tokens_ref.shape[0]
    block = count // 2
    width = router_ref.shape[0]
    units = weights_ref.shape[3]
    pair = 2 * units
    sub = min(block, TOKEN_ROWS)
    spans = [
        (part, low, part * block + low) for part in range(2) for low in range(0, block, sub)
    ]
    token_copies = [
        pltpu.make_async_copy(
            piece,
            tokens_ref.at[
                pl.ds(row, piece.shape[0]), pl.ds(column * width, piece.shape[1])
            ],
            token_sems.at[place],
        )
        for place, (piece, (row, column)) in enumerate(zip(token_pieces, token_places))
    ]

    def copy_in(piece, member, to_slot):
        return pltpu.make_async_copy(
            pieces[piece],
            weights_ref.at[to_slot, :, member, pl.ds(0, size), :],
            copy_sems.at[to_slot, member],
        )

    def copy_out(from_slot, member, owner):
        return pltpu.make_async_copy(
            made_ref.at[from_slot, member, :, pl.ds(0, size), :],
            grads_ref.at[owner],
            out_sems.at[from_slot, member],
        )

    @pl.when(step == 0)
    def begin():
        if size < units:
            weights_ref[...] = jnp.zeros_like(weights_ref)
        copy_in(0, 0, 0).start()
        copy_in(1, 1, 0).start()
        for token_copy in token_copies:
            token_copy.start()
        for sum_ref in sum_refs:
            sum_ref[...] = jnp.zeros_like(sum_ref)
        for token_copy in token_copies:
            token_copy.wait()
        for part, low, base in spans:
            picked = tokens_ref[pl.ds(base, sub), 2 * width :].astype(jnp.float32)
            logits = jnp.dot(
                tokens_ref[pl.ds(base, sub), :width],
                router_ref[...],
                preferred_element_type=jnp.float32,
            )
            masked = jnp.where(picked > 0.0, logits, -1e30)
            powers = jnp.exp(masked - jnp.max(masked, axis=1, keepdims=True)) * picked
            gates_ref[pl.ds(base, sub), :] = powers / jnp.sum(powers, axis=1, keepdims=True)

    for later in range(1, step_count):

        @pl.when(step == later - 1)
        def fetch(later=later):
            copy_in(2 * later, 0, later % 2).start()
            copy_in(2 * later + 1, 1, later % 2).start()

    for member in range(2):
        copy_in(0, member, slot).wait()

    firsts = [first_ref[2 * step + member] for member in range(2)]
    lane = lax.broadcasted_iota(jnp.int32, (sub, LANES), 1)
    heres = [(lane >= first) & (lane < first + local_experts) for first in firsts]

    def fold(values):
        shift = local_experts
        while shift < LANES:
            values = values + pltpu.roll(values, shift, 1)
            shift *= 2
        return values

    gate_up = weights_ref[slot, pl.ds(0, 2)].reshape(2 * pair, width)
    down = weights_ref[slot, 2].reshape(pair, width)
    for part, low, base in spans:
        span = pl.ds(base, sub)
        rows = tokens_ref[span, :width]
        cot = tokens_ref[span, width : 2 * width]
        gates = gates_ref[span, :]
        unit_gates = jnp.concatenate(
            [
                part_gates
                for here in heres
                for part_gates in [fold(jnp.where(here, gates, 0.0))] * (units // LANES)
            ],
            axis=1,
        )
        lin = dot_rows(rows, gate_up)
        gate_part, up_part = lin[:, :pair], lin[:, pair:]
        cot_active = dot_rows(cot, down)
        sigma = jax.nn.sigmoid(gate_part)
        silu = gate_part * sigma
        active = silu * up_part
        gated = (active * unit_gates).astype(jnp.bfloat16)
        products = active * cot_active
        for member, here in enumerate(heres):
            summed = 0.0
            for place in range(member * units, (member + 1) * units, LANES):
                summed = summed + products[:, place : place + LANES]
            gate_grads_ref[span, :] += jnp.where(here, fold(summed), 0.0)
        grad_active = cot_active * unit_gates
        grad_up = (grad_active * silu).astype(jnp.bfloat16)
        grad_gate = (grad_active * up_part * (sigma + silu * (1.0 - sigma))).astype(
            jnp.bfloat16
        )
        grad_lin = jnp.concatenate([grad_gate, grad_up], axis=1)
        lin_grads_ref[span, pl.ds(0, 2 * pair)] = grad_lin
        lin_grads_ref[span, pl.ds(2 * pair, pair)] = gated
        mixture_sum_ref[span, :] += jnp.dot(gated, down, preferred_element_type=jnp.float32)
        grad_sum_ref[span, :] += jnp.dot(
            grad_lin, gate_up, preferred_element_type=jnp.float32
        )

    @pl.when(step >= 2)
    def reuse():
        for member in range(2):
            copy_out(slot, member, 0).wait()

    def weight_grad(column, columns, side):
        return dot_tokens(
            lin_grads_ref[:, pl.ds(column, columns)],
            tokens_ref[:, side * width : (side + 1) * width],
        ).astype(jnp.bfloat16)

    for kind in range(3):
        made = weight_grad(kind * pair, pair, int(kind == 2))
        for member in range(2):
            made_ref[slot, member, kind] = made[member * units : (member + 1) * units]
    for member in range(2):
        copy_out(slot, member, owner_ref[2 * step + member]).start()

    @pl.when(step == step_count - 1)
    def finish():
        mixture_refs, grad_rows_refs, grad_router_ref = outs[:2], outs[2:4], outs[4]
        total = jnp.zeros(grad_router_ref.shape, jnp.float32)
        for part, low, base in spans:
            span = pl.ds(base, sub)
            gates = gates_ref[span, :]
            gate_grads = gate_grads_ref[span, :]
            mean_grad = jnp.sum(gates * gate_grads, axis=1, keepdims=True)
            logit_grads = gates * (gate_grads - mean_grad)
            coarse = logit_grads.astype(jnp.bfloat16).astype(jnp.float32)
            logit_pair = (coarse + pltpu.roll(logit_grads - coarse, LANES // 2, 1)).astype(
                jnp.bfloat16
            )
            mixture_refs[part][pl.ds(low, sub), :] = mixture_sum_ref[span, :].astype(jnp.bfloat16)
            grad_rows_refs[part][pl.ds(low, sub), :] = (
                grad_sum_ref[span, :] + dot_rows(logit_pair, router_ref[...])
            ).astype(jnp.bfloat16)
            total = total + dot_tokens(logit_pair, tokens_ref[span, :width])
        grad_router_ref[...] = total
        for member in range(2):
            copy_out(slot, member, 0).wait()
        if step_count > 1:
            for member in range(2):
                copy_out(1 - slot, member, 0).wait()


def experts_of_rows(token_pieces, token_places, count, router, arrays, where, firsts, owners, local_experts):
    block = count // 2
    width = router.shape[0]
    piece_count = len(where)
    size = arrays[0].shape[2]
    units = -(-size // LANES) * LANES
    anywhere = pl.BlockSpec(memory_space=pl.ANY)
    whole = lambda shape: pl.BlockSpec(
        shape, lambda *indices: (0,) * len(shape), pipeline_mode=pl.Buffered(1)
    )
    return pl.pallas_call(
        lambda *refs: expert_kernel(
            local_experts, size, where, len(arrays), token_places, refs
        ),
        grid_spec=pltpu.PrefetchScalarGridSpec(
            num_scalar_prefetch=2,
            grid=(piece_count // 2,),
            in_specs=[
                whole((width, LANES)),
            ]
            + [anywhere] * (len(token_pieces) + len(arrays)),
            out_specs=[whole((block, width))] * 4 + [whole((LANES, width)), anywhere],
            scratch_shapes=[
                pltpu.VMEM((count, LANES), jnp.float32),
                pltpu.VMEM((count, LANES), jnp.float32),
                pltpu.VMEM((count, width), jnp.float32),
                pltpu.VMEM((count, width), jnp.float32),
                pltpu.VMEM((2, 3, 2, units, width), jnp.bfloat16),
                pltpu.VMEM((count, 6 * units), jnp.bfloat16),
                pltpu.VMEM((2, 2, 3, units, width), jnp.bfloat16),
                pltpu.VMEM((count, 2 * width + LANES), jnp.bfloat16),
                pltpu.SemaphoreType.DMA((2, 2)),
                pltpu.SemaphoreType.DMA((2, 2)),
                pltpu.SemaphoreType.DMA((len(token_pieces),)),
            ],
        ),
        out_shape=[
            *[jax.ShapeDtypeStruct((block, width), jnp.bfloat16)] * 4,
            jax.ShapeDtypeStruct((LANES, width), jnp.float32),
            jax.ShapeDtypeStruct((piece_count, 3, size, width), jnp.bfloat16),
        ],
        compiler_params=pltpu.CompilerParams(
            dimension_semantics=("arbitrary",), vmem_limit_bytes=60 * 2**20
        ),
        cost_estimate=pl.CostEstimate(
            flops=18 * count * piece_count * units * width,
            bytes_accessed=piece_count * units * width * 12 + count * width * 16,
            transcendentals=count * piece_count * units,
        ),
    )(firsts, owners, router, *token_pieces, *arrays)


def spread_sums(parts, places, piece_count, shapes):
    held_rows, columns = parts[0][0].shape
    part_rows = held_rows * len(parts[0])
    rows = part_rows // piece_count
    upper = shapes[0][0] // 2
    lower = shapes[3][0]
    per_part = (part_rows - upper) // lower

    def kernel(places_ref, *refs):
        inputs, outputs, held_ref = refs[:-5], refs[-5:-1], refs[-1]
        for part in range(2):
            for place in range(len(parts[0])):
                held_ref[pl.ds(place * held_rows, held_rows), :] = inputs[
                    part * len(parts[0]) + place
                ][...].astype(jnp.float32)
            own = places_ref[part]

            def taken(low, high):
                pieces = []
                for piece in range(low // rows, -(-high // rows)):
                    start = pl.multiple_of((own ^ piece) * rows, 8)
                    whole_piece = held_ref[pl.ds(start, rows), :]
                    pieces.append(
                        whole_piece[
                            max(low - piece * rows, 0) : min(high - piece * rows, rows)
                        ]
                    )
                return jnp.concatenate(pieces, axis=0)

            top = taken(0, upper)
            at = 0
            for output in outputs[:3]:
                wide = output.shape[1]
                output[pl.ds(part * upper, upper), :] = top[:, at : at + wide]
                at += wide
            for place in range(per_part):
                start = upper + place * lower
                column = (part * per_part + place) * columns
                outputs[3][:, pl.ds(column, columns)] = taken(start, start + lower)

    inputs = [piece for part in parts for piece in part]
    whole = pl.BlockSpec(memory_space=pltpu.VMEM)
    return pl.pallas_call(
        kernel,
        in_specs=[pl.BlockSpec(memory_space=pltpu.SMEM)] + [whole] * len(inputs),
        out_specs=[whole] * 4,
        out_shape=[jax.ShapeDtypeStruct(shape, jnp.float32) for shape in shapes],
        scratch_shapes=[pltpu.VMEM((part_rows, columns), jnp.float32)],
        compiler_params=pltpu.CompilerParams(vmem_limit_bytes=32 * 2**20),
        cost_estimate=pl.CostEstimate(
            flops=0, bytes_accessed=12 * part_rows * columns, transcendentals=0
        ),
    )(places, *inputs)


def spread_units(sums, gate_up_shape, down_shape):
    unit_rows, local_experts, width = down_shape
    if local_experts % 8:
        sums = sums.reshape(2, 3, unit_rows // 2, local_experts, width).astype(jnp.float32)
        grad_gate_up = jnp.moveaxis(sums[:, :2], 1, 2).reshape(gate_up_shape)
        return grad_gate_up, sums[:, 2].reshape(down_shape)
    split = 4
    block = unit_rows // 2 // split

    def kernel(sums_ref, gate_up_ref, down_ref):
        shape = (block, local_experts, width)
        for kind in range(2):
            gate_up_ref[:, kind] = sums_ref[0, kind].astype(jnp.float32).reshape(shape)
        down_ref[...] = sums_ref[0, 2].astype(jnp.float32).reshape(shape)

    return pl.pallas_call(
        kernel,
        grid=(2 * split,),
        in_specs=[
            pl.BlockSpec(
                (1, 3, block * local_experts, width),
                lambda step: (step // split, 0, step % split, 0),
            )
        ],
        out_specs=[
            pl.BlockSpec((block, 2, local_experts, width), lambda step: (step, 0, 0, 0)),
            pl.BlockSpec((block, local_experts, width), lambda step: (step, 0, 0)),
        ],
        out_shape=[
            jax.ShapeDtypeStruct(gate_up_shape, jnp.float32),
            jax.ShapeDtypeStruct(down_shape, jnp.float32),
        ],
        compiler_params=pltpu.CompilerParams(
            dimension_semantics=("arbitrary",), vmem_limit_bytes=32 * 2**20
        ),
        cost_estimate=pl.CostEstimate(
            flops=0, bytes_accessed=18 * unit_rows * local_experts * width, transcendentals=0
        ),
    )(sums)


def on_device(
    tokens,
    gain_attn,
    gain_ffn,
    w_query,
    w_key,
    w_value,
    w_out,
    w_router,
    expert_gate_up,
    expert_down,
    segments,
    routes,
    cotangent,
):
    row_count, model_width = tokens.shape
    top_count = routes.shape[1]
    expert_count = w_router.shape[1]
    query_heads = w_query.shape[1] // HD
    kv_heads = w_key.shape[1] // HD
    group_size = query_heads // kv_heads
    scale = HD ** (-0.5)
    highest = lax.Precision.HIGHEST
    source = tokens.astype(jnp.float32)
    scale_attn = rms_scale(source)
    normed = (source * scale_attn * gain_attn).astype(jnp.bfloat16)
    tensor_step, expert_step, far, near = axis_steps()
    tensor_order = [tensor_step]
    token_order = [tensor_step, near]
    expert_masks, far_masks = (0,) + expert_step[1], (0,) + far[1]
    partners = [(mask, other) for other in far_masks for mask in expert_masks]

    expert_ids = jnp.arange(expert_count, dtype=jnp.int32)
    picks = jnp.sum(
        (routes[:, :, None] == expert_ids[None, None, :]).astype(jnp.bfloat16), axis=1
    )
    cot_picks = jnp.concatenate(
        [cotangent, picks, jnp.zeros((row_count, LANES - expert_count), jnp.bfloat16)], axis=1
    )
    unit_rows, local_experts = expert_down.shape[:2]
    half = unit_rows // 2
    units = half * local_experts
    expert_parts = []
    for low in (0, half):
        taken = expert_gate_up[low : low + half]
        expert_parts.append(
            jnp.stack(
                [taken[:, 0], taken[:, 1], expert_down[low : low + half]], axis=0
            ).reshape(1, 3, units, model_width)
        )
    first_parts = [
        [part] + [swap(part, axis, mask) for mask in masks[1:]]
        for part, axis, masks in zip(
            expert_parts, ("expert", "dp"), (expert_masks, far_masks)
        )
    ]
    dp_size, expert_size = lax.axis_size("dp"), lax.axis_size("expert")
    unused = jnp.zeros((model_width, LANES // 2 - expert_count), jnp.bfloat16)
    router_pair = jnp.concatenate([w_router, unused, w_router, unused], axis=1)

    (sequence,) = gather_parts([normed], [tensor_order])
    sequence, cot_picks, router_pair = lax.optimization_barrier(
        (sequence, cot_picks, router_pair)
    )
    first_mask, later_masks = tensor_step[1][0], tensor_step[1][1:]
    cot_first = swap(cot_picks, "tensor", first_mask)
    length = sequence.shape[0]
    positions = positions_of(segments[0])
    segment_row = in_held_order(segments[0], tensor_order, row_count)
    cosine, sine = rotary_tables(in_held_order(positions, tensor_order, row_count), HD)
    query_lin = jnp.dot(sequence, w_query, preferred_element_type=jnp.float32).reshape(
        length, query_heads, HD
    )
    key_lin = jnp.dot(sequence, w_key, preferred_element_type=jnp.float32).reshape(
        length, kv_heads, HD
    )
    values = (
        jnp.dot(sequence, w_value, preferred_element_type=jnp.float32)
        .astype(jnp.bfloat16)
        .reshape(length, kv_heads, HD)
    )
    queries = (
        rotate(query_lin, cosine, sine)
        .astype(jnp.bfloat16)
        .reshape(length, kv_heads, group_size, HD)
    )
    keys = rotate(key_lin, cosine, sine).astype(jnp.bfloat16)
    places = in_held_order(
        jnp.arange(length, dtype=jnp.int32), tensor_order, row_count
    )

    def block_scores(offset):
        block_rows = lax.dynamic_slice_in_dim(queries, offset, QBLK, 0)
        row_places = lax.dynamic_slice_in_dim(places, offset, QBLK, 0)
        row_segments = lax.dynamic_slice_in_dim(segment_row, offset, QBLK, 0)
        allowed = (row_segments[:, None] == segment_row[None, :]) & (
            places[None, :] <= row_places[:, None]
        )
        scores = (
            jnp.einsum("qkgd,skd->kgqs", block_rows, keys, preferred_element_type=jnp.float32)
            * scale
        )
        return (block_rows, jnp.where(allowed, scores, -1e30))

    def forward_block(block_index):
        block_rows, masked = block_scores(block_index * QBLK)
        peak = jnp.max(masked, axis=-1, keepdims=True)
        shifted = jnp.exp(masked - peak)
        summed = jnp.sum(shifted, axis=-1, keepdims=True)
        weights = (shifted / summed).astype(jnp.bfloat16)
        mixed_block = jnp.einsum(
            "kgqs,skd->qkgd", weights, values, preferred_element_type=jnp.float32
        )
        return (mixed_block.astype(jnp.bfloat16), (peak + jnp.log(summed))[..., 0])

    block_ids = jnp.arange(length // QBLK, dtype=jnp.int32)
    mixed_blocks, log_totals = lax.map(forward_block, block_ids)
    rooms = [
        jnp.zeros((len(parts),) + parts[0].shape[1:], jnp.bfloat16).at[0].set(parts[0][0])
        for parts in first_parts
    ]
    mixed, cot_first, rooms = tie(
        mixed_blocks.reshape(length, query_heads * HD), cot_first, rooms
    )
    attended_parts = jnp.dot(mixed, w_out, preferred_element_type=jnp.float32)
    kept, arrived = send_sums([attended_parts], [tensor_order], 0)
    arrived = arrived[0]
    arrived[0], first_parts = tie(arrived[0], first_parts)
    joined_parts = []
    for room, parts in zip(rooms, first_parts):
        for place, part in list(enumerate(parts))[1:]:
            room = lax.dynamic_update_slice_in_dim(room, part, place, 0)
        joined_parts.append(room)
    arrived[1:], unused_parts = tie(arrived[1:], joined_parts)
    attended = added([kept[0]] + arrived)
    weight_arrays, where = [], [{}, {}]
    for side, (masks, next_axis, next_masks) in enumerate(
        ((expert_masks, "dp", far_masks), (far_masks, "expert", expert_masks))
    ):
        name = lambda mask, other: (mask, other) if side == 0 else (other, mask)
        for mask, part in zip(masks, first_parts[side]):
            where[side][name(mask, 0)] = (len(weight_arrays), 0)
            weight_arrays.append(part)
        joined = joined_parts[side]
        for other in next_masks[1:]:
            for index, mask in enumerate(masks):
                where[side][name(mask, other)] = (len(weight_arrays), index)
            weight_arrays.append(swap(joined, next_axis, other))
    hidden = source + attended
    scale_ffn = rms_scale(hidden)
    normed_ffn = (hidden * scale_ffn * gain_ffn).astype(jnp.bfloat16)
    own_tokens = jnp.concatenate([normed_ffn, cot_picks], axis=1)
    arrived = [swap(normed_ffn, "tensor", first_mask)] + [
        swap(own_tokens, "tensor", mask) for mask in later_masks
    ]
    (arrived,) = tie(arrived)
    near_pieces = [normed_ffn, cot_picks, arrived[0], cot_first] + arrived[1:]
    near_places = [(0, 0), (0, 1), (row_count, 0), (row_count, 1)] + [
        (place * row_count, 0) for place in range(2, len(tensor_step[1]) + 1)
    ]
    pair_rows = (len(tensor_step[1]) + 1) * row_count
    token_pieces = near_pieces + [swap(piece, "dp", 1) for piece in near_pieces]
    token_places = near_places + [(row + pair_rows, column) for row, column in near_places]
    held, firsts, owners = [], [], []
    for mask, other in partners:
        owner_expert = lax.axis_index("expert") ^ mask
        owner_place = (lax.axis_index("dp") ^ other) // 2
        for side in range(2):
            held.append(where[side][mask, other])
            firsts.append(owner_expert * local_experts)
            owners.append((owner_place * expert_size + owner_expert) * 2 + side)
    *mixture_part, grad_near, grad_far, grad_router_rows, grad_pieces = experts_of_rows(
        token_pieces,
        token_places,
        2 * pair_rows,
        router_pair,
        weight_arrays,
        held,
        jnp.stack(firsts).astype(jnp.int32),
        jnp.stack(owners).astype(jnp.int32),
        local_experts,
    )
    groups = [
        [
            place * expert_size + other
            for place in range(start, dp_size, 2)
            for other in range(expert_size)
        ]
        for start in range(2)
    ]
    grad_units = lax.psum_scatter(
        grad_pieces,
        ("dp", "expert"),
        scatter_dimension=0,
        tiled=True,
        axis_index_groups=groups,
    )
    near_rows = added([grad_near, swap(grad_far, "dp", 1)]).astype(jnp.bfloat16)
    grad_router = (
        grad_router_rows[:expert_count]
        + grad_router_rows[LANES // 2 : LANES // 2 + expert_count]
    )
    kept, arrived = send_sums([near_rows], [tensor_order], 0)
    grad_router = sum_over(grad_router, "dp", axis_masks("dp")[1:])
    arrived, grad_router = tie(arrived, grad_router)
    grad_normed_ffn = added([kept[0]] + arrived[0])
    grad_output = cotangent.astype(jnp.float32)
    grad_hidden_norm, grad_gain_ffn = norm_back(hidden, scale_ffn, gain_ffn, grad_normed_ffn)
    grad_hidden = grad_output + grad_hidden_norm
    attn_rows = grad_hidden.astype(jnp.bfloat16)
    arrived = send_parts([attn_rows], [tensor_order], 0)
    grad_router = sum_over(grad_router, "expert", axis_masks("expert"))
    arrived, grad_router = tie(arrived, grad_router)
    (attn_grad,) = take_parts([attn_rows], arrived)
    mixture_part, attn_grad, grad_router = tie(mixture_part, attn_grad, grad_router)
    mixture_rows = added([mixture_part[0], swap(mixture_part[1], "dp", 1)]).astype(
        jnp.bfloat16
    )
    tensor_masks = axis_masks("tensor")
    grad_w_out = jnp.einsum("lh,ld->hd", mixed, attn_grad, preferred_element_type=jnp.float32)
    grad_mixed = (
        jnp.einsum("ld,hd->lh", attn_grad, w_out, preferred_element_type=jnp.float32)
        .astype(jnp.bfloat16)
        .reshape(length, kv_heads, group_size, HD)
    )

    def backward_block(carried, scanned):
        key_sum, value_sum = carried
        block_index, log_block = scanned
        offset = block_index * QBLK
        block_rows, masked = block_scores(offset)
        probs = jnp.exp(masked - log_block[..., None])
        weights = probs.astype(jnp.bfloat16)
        grad_block = lax.dynamic_slice_in_dim(grad_mixed, offset, QBLK, 0)
        grad_probs = jnp.einsum(
            "qkgd,skd->kgqs", grad_block, values, preferred_element_type=jnp.float32
        )
        inner = jnp.sum(probs * grad_probs, axis=-1, keepdims=True)
        grad_scores = (probs * (grad_probs - inner)).astype(jnp.bfloat16)
        grad_query = (
            jnp.einsum("kgqs,skd->qkgd", grad_scores, keys, preferred_element_type=jnp.float32)
            * scale
        )
        key_sum = (
            key_sum
            + jnp.einsum(
                "kgqs,qkgd->skd", grad_scores, block_rows, preferred_element_type=jnp.float32
            )
            * scale
        )
        value_sum = value_sum + jnp.einsum(
            "kgqs,qkgd->skd", weights, grad_block, preferred_element_type=jnp.float32
        )
        return ((key_sum, value_sum), grad_query)

    zero_keys = jnp.zeros((length, kv_heads, HD), jnp.float32)
    (key_grads, value_grads), query_grads = lax.scan(
        backward_block, (zero_keys, zero_keys), (block_ids, log_totals)
    )
    grad_query_lin = (
        rotate_back(query_grads.reshape(length, query_heads, HD), cosine, sine)
        .astype(jnp.bfloat16)
        .reshape(length, query_heads * HD)
    )
    grad_key_lin = (
        rotate_back(key_grads, cosine, sine).astype(jnp.bfloat16).reshape(length, kv_heads * HD)
    )
    grad_value_lin = value_grads.astype(jnp.bfloat16).reshape(length, kv_heads * HD)
    grad_w_query = jnp.einsum(
        "ld,lh->dh", sequence, grad_query_lin, preferred_element_type=jnp.float32
    )
    grad_w_key = jnp.einsum("ld,lh->dh", sequence, grad_key_lin, preferred_element_type=jnp.float32)
    grad_w_value = jnp.einsum(
        "ld,lh->dh", sequence, grad_value_lin, preferred_element_type=jnp.float32
    )
    grad_sequence = (
        jnp.einsum("lh,dh->ld", grad_query_lin, w_query, preferred_element_type=jnp.float32)
        + jnp.einsum("lh,dh->ld", grad_key_lin, w_key, preferred_element_type=jnp.float32)
        + jnp.einsum("lh,dh->ld", grad_value_lin, w_value, preferred_element_type=jnp.float32)
    )
    sequence_rows = grad_sequence.astype(jnp.bfloat16)
    gain_sums = jnp.stack(
        [
            jnp.sum(grad_sequence * sequence.astype(jnp.float32), axis=0) / gain_attn,
            grad_gain_ffn,
        ]
    )
    columns = jnp.concatenate([grad_w_query, grad_w_key, grad_w_value], axis=1)
    sum_orders = [[expert_step, far, near], [far, expert_step, near]]
    sequence_count = lax.axis_size("dp") * lax.axis_size("expert")

    def reorder(parts):
        return [
            in_held_order(part, order, part.shape[0] // sequence_count)
            for part, order in zip(parts, sum_orders)
        ]

    sequence_rows, mixture_rows, columns, grad_w_out, gain_sums, grad_router = tie(
        sequence_rows, mixture_rows, columns, grad_w_out, gain_sums, grad_router
    )
    kept, arrived = send_sums([sequence_rows], [tensor_order], 0)
    arrived = arrived[0]
    blocks_out = jnp.split(grad_w_out, model_width // columns.shape[1], axis=1)
    block_rows, per_part = blocks_out[0].shape[0], len(blocks_out) // 2
    sums = reorder(
        [
            jnp.concatenate([upper] + lower, axis=0)
            for upper, lower in zip(
                jnp.split(columns, 2, axis=0), (blocks_out[:per_part], blocks_out[per_part:])
            )
        ]
    )
    for step in reversed(range(3)):
        sums_kept, sums_arrived = send_sums(sums, sum_orders, step)
        if step == 2:
            (sums_arrived,) = tie(sums_arrived)
        elif step == 1:
            sums_arrived, arrived[0] = tie(sums_arrived, arrived[0])
        else:
            sums_arrived, arrived, mixture_rows, gain_sums, grad_router = tie(
                sums_arrived, arrived, mixture_rows, gain_sums, grad_router
            )
        sums = take_sums(sums_kept, sums_arrived)
    mixture_kept, mixture_arrived = send_sums([mixture_rows], [tensor_order], 0)
    mixture_arrived = mixture_arrived[0]
    for step in range(3):
        sums_arrived = send_parts(sums, sum_orders, step)
        if step == 0:
            loose = sum_over(
                jnp.concatenate([grad_router, gain_sums], axis=0), "dp", axis_masks("dp")[:1]
            )
            gain_sums = sum_over(loose[expert_count:], "dp", axis_masks("dp")[1:])
            gain_sums = sum_over(gain_sums, "expert", axis_masks("expert"))
            loose = jnp.concatenate([loose[:expert_count], gain_sums], axis=0)
            sums_arrived, mixture_arrived, loose = tie(sums_arrived, mixture_arrived, loose)
        elif step == 1:
            loose = sum_over(loose, "tensor", tensor_masks[:1])
            sums_arrived, loose, grad_units = tie(sums_arrived, loose, grad_units)
        elif step == 2:
            loose = sum_over(loose, "tensor", tensor_masks[1:])
            sums_arrived, loose = tie(sums_arrived, loose)
            grad_router, gain_sums = loose[:expert_count].T, loose[expert_count:]
        if step < 2:
            sums = take_parts(sums, sums_arrived)
    grad_gain_attn, grad_gain_ffn = gain_sums[0], gain_sums[1]
    grad_w_query, grad_w_key, grad_w_value, grad_w_out = spread_sums(
        [[part] + pieces for part, pieces in zip(sums, sums_arrived)],
        jnp.stack([held_by(order) for order in sum_orders]).astype(jnp.int32),
        sequence_count,
        [w_query.shape, w_key.shape, w_value.shape, w_out.shape],
    )
    grad_normed = added([grad_sequence[:row_count]] + arrived)
    output = (hidden + added(mixture_kept + mixture_arrived)).astype(jnp.bfloat16)
    grad_source_norm, unused_gain = norm_back(source, scale_attn, gain_attn, grad_normed)
    grad_tokens = grad_hidden + grad_source_norm
    grad_gate_up, grad_down = spread_units(
        grad_units, expert_gate_up.shape, expert_down.shape
    )
    return (
        output,
        grad_tokens,
        grad_gain_attn,
        grad_gain_ffn,
        grad_w_query,
        grad_w_key,
        grad_w_value,
        grad_w_out,
        grad_router,
        grad_gate_up,
        grad_down,
    )


def solution(mesh):
    placed = (
        P(("dp", "expert", "tensor"), None),
        P(),
        P(),
        P(None, "tensor"),
        P(None, "tensor"),
        P(None, "tensor"),
        P("tensor", None),
        P(),
        P(("dp", "tensor"), None, "expert", None),
        P(("dp", "tensor"), "expert", None),
        P(("dp", "expert"), None),
        P(("dp", "expert", "tensor"), None),
        P(("dp", "expert", "tensor"), None),
    )
    return jax.shard_map(
        on_device,
        mesh=mesh,
        in_specs=placed,
        out_specs=(
            P(("dp", "expert", "tensor"), None),
            P(("dp", "expert", "tensor"), None),
            P(),
            P(),
            P(None, "tensor"),
            P(None, "tensor"),
            P(None, "tensor"),
            P("tensor", None),
            P(),
            P(("dp", "tensor"), None, "expert", None),
            P(("dp", "tensor"), "expert", None),
        ),
        check_vma=False,
    )
```
